32 devices in a mesh: grp: 2 (over x), row: 16 (over z, y, core).
Axes of the slice: x: 2, y: 2, z: 4, core: 2. Of those that a mesh axis runs over, the one named last changes fastest.
Arguments:
- object_strip: float32 [2, 8192, 1024], P(None, ('grp', 'row')), parts along dimension 1, may hold values from -6 to 6
- probe_store: float32 [32, 2, 2, 128, 128], P(('grp', 'row')), parts along dimension 0, may hold values from -5 to 5
- amplitudes: float32 [512, 128, 128], P(('grp', 'row')), parts along dimension 0, may hold values from 0.2 to 4
- scan_of: int32 [512], P(('grp', 'row')), parts along dimension 0, may hold values from 0 to 7
- offsets: int32 [512, 2], P(('grp', 'row')), parts along dimension 0, may hold values from 0 to 3968, as said below
- counts: int32 [32], P(('grp', 'row')), parts along dimension 0, may hold values from 1 to 16, 160 in all
- owner: int32 [16], P('grp'), parts along dimension 0, may hold values from 0 to 15, as said below
Outputs:
- new_object: float32 [2, 8192, 1024], P(None, ('grp', 'row')), parts along dimension 1
- new_probes: float32 [32, 2, 2, 128, 128], P(('grp', 'row')), parts along dimension 0
The draws below stay inside these ranges and needn't reach their ends.
There are 2 independent parts, one for each index of `grp`. The reference program is written for one: setup_inputs(seed, part) draws one part's arguments, and reference() takes and returns one part's arrays. A program takes and returns all parts, laid end to end along the dimension named above; each array names one. Nothing has to cross between parts.
Inputs may be any that keep to these rules, and one draw needn't show every extreme that they name: offsets[p, 0] is a window's first row and offsets[p, 1] its first column; the windows of device d's slots (p // 16 = d) start in rows d * 256 to (d + 1) * 256 - 1 and lie wholly inside the strip. Slots p mod 16 >= counts[p // 16] are not live. `owner`: the owners of the 8 scans are distinct devices.
All inputs are finite; a program needn't handle non-finite values. No bound on the sum of `counts` on one device may be relied on, other than what follows from the above.
Results may differ from the reference program's by a relative error of at most 0.0001.
Values sent between devices are 32-bit elements; how exact they have to be, the bound alone decides.
No kernel may reach another device: no remote copies, remote signals or barrier semaphores. Data moves between devices by JAX's collectives and lax.ppermute only.
A program may use at most 128 MiB of HBM per device.

```python
import math
import jax
import jax.numpy as jnp
import numpy as np
from jax import lax

P_SIZE = 128
MODES = 2
SCANS = 8
OW = 1024
TILE_ROWS = 256
SLOTS = 16
ROWS = 4096
POSITIONS = 256
N_ROW = 16


def draw_offsets(key, part):
    key_rows = jax.random.fold_in(key, 11)
    key_cols = jax.random.fold_in(key, 23)
    device = jnp.arange(POSITIONS, dtype=jnp.int32) // SLOTS
    slot_index = jnp.arange(POSITIONS, dtype=jnp.int32) % SLOTS
    row_limit = jnp.where(device == N_ROW - 1, TILE_ROWS - P_SIZE + 1, TILE_ROWS).astype(jnp.int32)
    row_local = jax.random.randint(key_rows, (POSITIONS,), 0, row_limit, dtype=jnp.int32)
    col_start = jax.random.randint(key_cols, (POSITIONS,), 0, OW - P_SIZE + 1, dtype=jnp.int32)
    first_last = (device == N_ROW - 1) & (slot_index == 0)
    first_first = (device == 0) & (slot_index == 0)
    row_local = jnp.where(first_last, TILE_ROWS - P_SIZE, row_local)
    row_local = jnp.where(first_first, 0, row_local)
    col_start = jnp.where(first_first, OW - P_SIZE, col_start)
    row_start = row_local + device * TILE_ROWS
    return jnp.stack([row_start, col_start], axis=1).astype(jnp.int32)


def draw_owner(key, part):
    inner = jax.random.permutation(jax.random.fold_in(key, 37), N_ROW - 2)[:SCANS - 2].astype(jnp.int32) + 1
    chosen = jnp.concatenate([jnp.zeros((1,), jnp.int32), jnp.full((1,), N_ROW - 1, jnp.int32), inner])
    order = jax.random.permutation(jax.random.fold_in(key, 41), SCANS)
    return chosen[order].astype(jnp.int32)


def set_ends(entries, rng, low, high):
    longest = entries.shape.index(max(entries.shape))
    spots = []
    for shift in (0, 1):
        where = [jax.random.randint(jax.random.fold_in(rng, axis), (), 0, length) for axis, length in enumerate(entries.shape)]
        where[longest] = (where[longest] + shift) % entries.shape[longest]
        spots.append(tuple(where))
    return entries.at[spots[0]].set(low).at[spots[1]].set(high)


def block_scale(stream_key, shape, split, least, high):
    def one(axis_at, parts):
        steps = jax.random.uniform(jax.random.fold_in(jax.random.fold_in(stream_key, 6), axis_at), (parts,), jnp.float32, least / len(split), high / len(split))
        return jnp.repeat(jnp.exp(steps), shape[axis_at] // parts).reshape((-1,) + (1,) * (len(shape) - axis_at - 1))

    gain = one(*split[0])
    for cut in split[1:]:
        gain = gain * one(*cut)
    return gain


def split_up(count, total, limit, slope):
    portions = [(1 << 20) // math.isqrt(grade ** slope) + 1 for grade in range(2, count + 1)]
    surplus, holding = total - limit - (count - 1), [1] * (count - 1)
    while surplus > 0:
        free = [i for i in range(count - 1) if holding[i] < limit]
        mass, left = sum([portions[i] for i in free]), surplus
        for i in free:
            more = min(limit - holding[i], max(1, left * portions[i] // mass), surplus)
            holding[i] = holding[i] + more
            surplus = surplus - more
    return np.array([limit] + holding)


def uneven(rng, number_of, total, most, lean):
    if number_of == 2:
        one = jax.random.randint(rng, (), max(1, total - most), min(most, total - 1) + 1)
        return jnp.stack([one, total - one])
    sizes = jnp.asarray(split_up(number_of, total, most, lean), jnp.int32)
    twos = (number_of - 1) // 2
    giver, sink = sizes[1:1 + 2 * twos:2], sizes[2:2 + 2 * twos:2]
    margin = jnp.minimum(giver - 1, most - sink)
    moved = jax.random.randint(jax.random.fold_in(rng, 1), (twos,), 0, 1 << 20) % (margin + 1)
    sizes = sizes.at[1:1 + 2 * twos:2].set(giver - moved).at[2:2 + 2 * twos:2].set(sink + moved)
    return sizes[jax.random.permutation(jax.random.fold_in(rng, 2), number_of)]


def noise(key, shape, deviation, bound, cuts=(), kind=jnp.bfloat16):
    level = block_scale(key, shape, cuts, -0.22, 0.18) if cuts else 1.0
    array = jax.random.normal(key, shape, jnp.float32) * deviation * level
    return jnp.minimum(jnp.maximum(array, -bound), bound).astype(kind)


def setup_inputs(seed: int = 0, part: int = 0) -> dict:
    streams_of = jax.random.split(jax.random.key(seed), 8)
    part_keys = jax.random.split(jax.random.fold_in(streams_of[7], part), 8)
    object_strip = noise(part_keys[0], (2, ROWS, OW), 1.0, 6.0, ((1, 16),), jnp.float32)
    probe_store = noise(part_keys[1], (N_ROW, MODES, 2, P_SIZE, P_SIZE), 0.7, 5.0, ((0, 16),), jnp.float32)
    amplitudes = jnp.clip(jnp.exp(math.log(4.0) - 2.9957323 * jax.random.uniform(part_keys[2], (POSITIONS, P_SIZE, P_SIZE), jnp.float32) ** block_scale(part_keys[2], (POSITIONS, P_SIZE, P_SIZE), ((0, 16),), -0.2, 0.2)), 0.2, 4.0)
    scan_of = set_ends(jax.random.randint(part_keys[3], (POSITIONS,), 0, SCANS), jax.random.fold_in(part_keys[3], 1), 0, SCANS - 1).astype(jnp.int32)
    offsets = draw_offsets(jax.random.fold_in(jax.random.fold_in(streams_of[7], part), 71), part)
    counts = uneven(part_keys[5], N_ROW, N_ROW * SLOTS * 5 // 8, SLOTS, 2).astype(jnp.int32)
    owner = draw_owner(jax.random.fold_in(jax.random.fold_in(streams_of[7], part), 71), part)
    return dict(object_strip=object_strip, probe_store=probe_store, amplitudes=amplitudes, scan_of=scan_of, offsets=offsets, counts=counts, owner=owner)


damping = 1.0
floor_level = 0.3

def reference(object_strip, probe_store, amplitudes, scan_of, offsets, counts, owner):
    obj = lax.complex(object_strip[0], object_strip[1])
    chosen = probe_store[owner]
    probes = lax.complex(chosen[:, :, 0], chosen[:, :, 1])
    obj_num = jnp.zeros_like(obj)
    obj_den = jnp.zeros(obj.shape, object_strip.dtype)
    probe_num = jnp.zeros_like(probes)
    probe_den = jnp.zeros((SCANS, P_SIZE, P_SIZE), object_strip.dtype)

    def visit(p, carry):
        obj_num, obj_den, probe_num, probe_den = carry
        p = jnp.asarray(p).astype(jnp.int32)
        live_flag = (p % SLOTS < counts[p // SLOTS]).astype(object_strip.dtype)
        row_start = offsets[p, 0]
        col_start = offsets[p, 1]
        window = lax.dynamic_slice(obj, (row_start, col_start), (P_SIZE, P_SIZE))
        scan_index = scan_of[p]
        probe_now = probes[scan_index]
        exit_wave = probe_now * window[None]
        spectrum = jnp.fft.fft2(exit_wave, norm='ortho')
        intensity = lax.optimization_barrier(jnp.sum(jnp.real(spectrum) ** 2 + jnp.imag(spectrum) ** 2, axis=0))
        magnitude = jnp.maximum(jnp.sqrt(intensity), floor_level)
        factor = amplitudes[p] / magnitude - 1.0
        change = jnp.fft.ifft2(factor[None] * spectrum, norm='ortho')
        obj_term = lax.optimization_barrier(jnp.sum(jnp.conj(probe_now) * change, axis=0)) * live_flag
        den_term = lax.optimization_barrier(jnp.sum(jnp.real(probe_now) ** 2 + jnp.imag(probe_now) ** 2, axis=0)) * live_flag
        current = lax.dynamic_slice(obj_num, (row_start, col_start), (P_SIZE, P_SIZE))
        obj_num = lax.dynamic_update_slice(obj_num, current + obj_term, (row_start, col_start))
        current_den = lax.dynamic_slice(obj_den, (row_start, col_start), (P_SIZE, P_SIZE))
        obj_den = lax.dynamic_update_slice(obj_den, current_den + den_term, (row_start, col_start))
        probe_term = jnp.conj(window)[None] * change * live_flag
        probe_num = probe_num.at[scan_index].add(probe_term)
        window_den = (jnp.real(window) ** 2 + jnp.imag(window) ** 2) * live_flag
        probe_den = probe_den.at[scan_index].add(window_den)
        return (obj_num, obj_den, probe_num, probe_den)
    obj_num, obj_den, probe_num, probe_den = lax.fori_loop(0, POSITIONS, visit, (obj_num, obj_den, probe_num, probe_den))
    updated = obj + obj_num / (obj_den + damping)
    new_object = jnp.stack([jnp.real(updated), jnp.imag(updated)], axis=0)
    fresh = probes + probe_num / (probe_den[:, None] + damping)
    fresh_parts = jnp.stack([jnp.real(fresh), jnp.imag(fresh)], axis=2)
    new_probes = probe_store.at[owner].set(fresh_parts)
    return (new_object, new_probes)
```

```python
import functools
import math

import jax
import jax.numpy as jnp
import numpy as np
from jax import lax
from jax.experimental import pallas as pl
from jax.experimental.pallas import tpu as pltpu
from jax.sharding import PartitionSpec as P

damping = 1.0
floor_level = 0.3
LANES = 128
SLOTS_AT_ONCE = 2
VMEM_BYTES = 48 * 1024 * 1024


def moved(block, distance):
    size = lax.axis_size("row")
    return lax.ppermute(block, "row", [(i, i + distance) for i in range(size) if 0 <= i + distance < size])


def swapped(block, mask):
    return lax.ppermute(block, "row", [(i, i ^ mask) for i in range(lax.axis_size("row"))])


def split(value):
    high = value.astype(jnp.bfloat16)
    low = (value - high.astype(jnp.float32)).astype(jnp.bfloat16)
    return high, low


def transform_tables(points):
    index = np.arange(points)
    angle = (index[:, None] * index[None, :] % points) * (2.0 * math.pi / points)
    cos, sin = np.cos(angle) / math.sqrt(points), np.sin(angle) / math.sqrt(points)
    minus = np.block([[cos, -sin], [sin, cos]])
    plus = np.block([[cos, sin], [-sin, cos]])

    def parts(matrix, axis):
        matrix = matrix.astype(np.float32)
        high = matrix.astype(jnp.bfloat16)
        low = (matrix - high.astype(np.float32)).astype(jnp.bfloat16)
        return jnp.asarray(np.concatenate([high, high, low], axis=axis))

    return parts(minus, 0), parts(plus, 1), parts(minus, 1), parts(plus, 0)


def right_product(rows, table):
    high, low = split(rows)
    return jnp.dot(jnp.concatenate([high, low, high], axis=1), table, preferred_element_type=jnp.float32)


def left_product(table, columns):
    high, low = split(columns)
    return jnp.dot(table, jnp.concatenate([high, low, high], axis=0), preferred_element_type=jnp.float32)


def update_kernel(dims, meta, slot_of, live, amplitudes, obj, rim, right_f, left_f, left_i, right_i, *rest):
    piece_sizes, group_sizes, slots = dims
    pieces = rest[: len(piece_sizes)]
    rest = rest[len(piece_sizes) :]
    num_top, num_low, squares = rest[:3]
    groups = rest[3 : 3 + len(group_sizes)]
    table, ext, acc, part, piece_sems, out_sems = rest[3 + len(group_sizes) :]
    points = LANES
    tile_rows = obj.shape[1]
    blocks = obj.shape[2] // LANES
    modes = table.shape[1] // 2

    copies = []
    at = 0
    for k, size in enumerate(piece_sizes):
        copies.append(pltpu.make_async_copy(pieces[k], table.at[pl.ds(at, size)], piece_sems.at[k]))
        at += size
    for copy in copies:
        copy.start()
    for b in range(blocks):
        ext[:, b, :tile_rows, :] = obj[:, :, b * LANES : (b + 1) * LANES]
        ext[:, b, tile_rows:, :] = rim[:, :, b * LANES : (b + 1) * LANES]
    ext[:, blocks] = jnp.zeros_like(ext[:, blocks])
    acc[...] = jnp.zeros_like(acc)
    part[...] = jnp.zeros_like(part)
    for copy in copies:
        copy.wait()
    for s in range(squares.shape[0]):
        probe = table[slot_of[s]]
        squares[s] = jnp.sum(probe * probe, axis=0)

    lane = lax.broadcasted_iota(jnp.int32, (points, LANES), 1)
    count = live[0]

    def step(i, carry):
        wins, probes, places, waves, flags = [], [], [], [], []
        for u in range(SLOTS_AT_ONCE):
            p = i * SLOTS_AT_ONCE + u
            flags.append((p < count).astype(jnp.float32))
            row, col, scan = meta[4 * p], meta[4 * p + 1], meta[4 * p + 2]
            slot = slot_of[scan]
            block, shift = col // LANES, col % LANES
            back = lax.rem(LANES - shift, LANES)
            keep = lane < LANES - shift
            win = []
            for ch in range(2):
                first = pltpu.roll(ext[ch, block, pl.ds(row, points), :], back, 1)
                second = pltpu.roll(ext[ch, block + 1, pl.ds(row, points), :], back, 1)
                win.append(jnp.where(keep, first, second))
            probe = [(table[slot, 2 * m], table[slot, 2 * m + 1]) for m in range(modes)]
            for pr, pi in probe:
                waves.append(
                    jnp.concatenate([pr * win[0] - pi * win[1], pr * win[1] + pi * win[0]], axis=1)
                )
            wins.append(win)
            probes.append(probe)
            places.append((p, row, block, shift, slot))
        half = right_product(jnp.concatenate(waves, axis=0), right_f[...])
        columns = []
        for k in range(SLOTS_AT_ONCE * modes):
            rows = half[k * points : (k + 1) * points]
            columns.append(jnp.concatenate([rows[:, :points], rows[:, points:]], axis=0))
        spec = left_product(left_f[...], jnp.concatenate(columns, axis=1))
        columns = []
        for u in range(SLOTS_AT_ONCE):
            own = [spec[:, (u * modes + m) * points : (u * modes + m + 1) * points] for m in range(modes)]
            total = functools.reduce(jnp.add, [s * s for s in own])
            intensity = total[:points] + total[points:]
            factor = amplitudes[places[u][0]] * lax.rsqrt(jnp.maximum(intensity, floor_level * floor_level)) - 1.0
            factor = factor * flags[u]
            factor = jnp.concatenate([factor, factor], axis=0)
            columns += [s * factor for s in own]
        half = left_product(left_i[...], jnp.concatenate(columns, axis=1))
        rows = []
        for k in range(SLOTS_AT_ONCE * modes):
            column = half[:, k * points : (k + 1) * points]
            rows.append(jnp.concatenate([column[:points], column[points:]], axis=1))
        change = right_product(jnp.concatenate(rows, axis=0), right_i[...])
        for u in range(SLOTS_AT_ONCE):
            p, row, block, shift, slot = places[u]
            wr, wi = wins[u]
            term_r = term_i = None
            for m in range(modes):
                k = u * modes + m
                pr, pi = probes[u][m]
                dr = change[k * points : (k + 1) * points, :points]
                di = change[k * points : (k + 1) * points, points:]
                tr, ti = pr * dr + pi * di, pr * di - pi * dr
                term_r = tr if m == 0 else term_r + tr
                term_i = ti if m == 0 else term_i + ti
                part[slot, 2 * m] += wr * dr + wi * di
                part[slot, 2 * m + 1] += wr * di - wi * dr
            part[slot, 2 * modes] += (wr * wr + wi * wi) * flags[u]
            first = lane >= shift
            for ch, term in enumerate((term_r, term_i)):
                term = pltpu.roll(term, shift, 1)
                acc[ch, block, pl.ds(row, points), :] += jnp.where(first, term, 0.0)
                acc[ch, block + 1, pl.ds(row, points), :] += jnp.where(first, 0.0, term)
        return carry

    lax.fori_loop(0, (count + SLOTS_AT_ONCE - 1) // SLOTS_AT_ONCE, step, 0)

    copies = []
    at = 0
    for k, size in enumerate(group_sizes):
        copies.append(pltpu.make_async_copy(part.at[pl.ds(at, size)], groups[k], out_sems.at[k]))
        at += size
    k = len(group_sizes)
    copies.append(
        pltpu.make_async_copy(acc.at[:, pl.ds(0, blocks), pl.ds(tile_rows, points), :], num_low, out_sems.at[k])
    )
    copies.append(
        pltpu.make_async_copy(acc.at[:, pl.ds(0, blocks), pl.ds(0, tile_rows), :], num_top, out_sems.at[k + 1])
    )
    for copy in copies:
        copy.start()
    for copy in copies:
        copy.wait()


def update(meta, slot_of, live, amplitudes, obj, rim, tables, pieces, group_sizes):
    points = amplitudes.shape[-1]
    tile_rows = obj.shape[1]
    blocks = obj.shape[2] // LANES
    channels = pieces[0].shape[1]
    scans = slot_of.shape[0]
    piece_sizes = tuple(piece.shape[0] for piece in pieces)
    slots = sum(piece_sizes)
    f32 = jnp.float32
    smem = pl.BlockSpec(memory_space=pltpu.SMEM)
    vmem = pl.BlockSpec(memory_space=pltpu.VMEM)
    anywhere = pl.BlockSpec(memory_space=pl.ANY)
    return pl.pallas_call(
        functools.partial(update_kernel, (piece_sizes, group_sizes, slots)),
        out_shape=[
            jax.ShapeDtypeStruct((2, blocks, tile_rows, LANES), f32),
            jax.ShapeDtypeStruct((2, blocks, points, LANES), f32),
            jax.ShapeDtypeStruct((scans, points, points), f32),
        ]
        + [jax.ShapeDtypeStruct((size, channels + 1, points, points), f32) for size in group_sizes],
        in_specs=[smem] * 3 + [vmem] * 7 + [anywhere] * len(pieces),
        out_specs=[anywhere, anywhere, vmem] + [anywhere] * len(group_sizes),
        scratch_shapes=[
            pltpu.VMEM((slots, channels, points, points), f32),
            pltpu.VMEM((2, blocks + 1, tile_rows + points, LANES), f32),
            pltpu.VMEM((2, blocks + 1, tile_rows + points, LANES), f32),
            pltpu.VMEM((slots, channels + 1, points, points), f32),
            pltpu.SemaphoreType.DMA((len(pieces),)),
            pltpu.SemaphoreType.DMA((len(group_sizes) + 2,)),
        ],
        compiler_params=pltpu.CompilerParams(vmem_limit_bytes=VMEM_BYTES),
        cost_estimate=pl.CostEstimate(flops=6 * 10**9, bytes_accessed=16 * 2**20, transcendentals=2**18),
        name="update",
    )(meta, slot_of, live, amplitudes, obj, rim, *tables, *pieces)


def density_kernel(tile_rows, meta, above, squares, density, ext):
    points = LANES
    blocks = density.shape[0]
    ext[...] = jnp.zeros_like(ext)
    lane = lax.broadcasted_iota(jnp.int32, (points, LANES), 1)

    def place(values, row, col):
        block, shift = col // LANES, col % LANES
        first = lane >= shift
        values = pltpu.roll(values, shift, 1)
        ext[block, pl.ds(row, points), :] += jnp.where(first, values, 0.0)
        ext[block + 1, pl.ds(row, points), :] += jnp.where(first, 0.0, values)

    def own(p, carry):
        @pl.when(meta[4 * p + 3] > 0)
        def _():
            place(squares[meta[4 * p + 2]], meta[4 * p] + points, meta[4 * p + 1])

        return carry

    def upper(p, carry):
        row = above[4 * p] - tile_rows + points

        @pl.when((above[4 * p + 3] > 0) & (row > 0))
        def _():
            place(squares[above[4 * p + 2]], row, above[4 * p + 1])

        return carry

    lax.fori_loop(0, meta.shape[0] // 4, own, 0)
    lax.fori_loop(0, above.shape[0] // 4, upper, 0)
    density[...] = ext[:blocks, points : points + tile_rows, :]


def density_of(meta, above, squares, tile_rows, blocks):
    points = squares.shape[-1]
    smem = pl.BlockSpec(memory_space=pltpu.SMEM)
    vmem = pl.BlockSpec(memory_space=pltpu.VMEM)
    return pl.pallas_call(
        functools.partial(density_kernel, tile_rows),
        out_shape=jax.ShapeDtypeStruct((blocks, tile_rows, LANES), jnp.float32),
        in_specs=[smem, smem, vmem],
        out_specs=vmem,
        scratch_shapes=[pltpu.VMEM((blocks + 1, points + tile_rows + points, LANES), jnp.float32)],
        compiler_params=pltpu.CompilerParams(vmem_limit_bytes=VMEM_BYTES),
        cost_estimate=pl.CostEstimate(flops=2**23, bytes_accessed=8 * 2**20, transcendentals=0),
        name="density",
    )(meta, above, squares)


def finish_kernel(obj, num_top, received, density, out):
    points = received.shape[2]
    for b in range(density.shape[0]):
        columns = slice(b * LANES, (b + 1) * LANES)
        scale = 1.0 / (density[b] + damping)
        for ch in range(2):
            head = num_top[ch, b, :points] + received[ch, b]
            out[ch, :points, columns] = obj[ch, :points, columns] + head * scale[:points]
            out[ch, points:, columns] = obj[ch, points:, columns] + num_top[ch, b, points:] * scale[points:]


def finish(obj, num_top, received, density):
    vmem = pl.BlockSpec(memory_space=pltpu.VMEM)
    return pl.pallas_call(
        finish_kernel,
        out_shape=jax.ShapeDtypeStruct(obj.shape, obj.dtype),
        in_specs=[vmem] * 4,
        out_specs=vmem,
        compiler_params=pltpu.CompilerParams(vmem_limit_bytes=VMEM_BYTES),
        cost_estimate=pl.CostEstimate(flops=2**21, bytes_accessed=8 * 2**20, transcendentals=0),
        name="finish",
    )(obj, num_top, received, density)


def local(object_strip, probe_store, amplitudes, scan_of, offsets, counts, owner):
    device = lax.axis_index("row")
    size = lax.axis_size("row")
    tile_rows = object_strip.shape[1]
    blocks = object_strip.shape[2] // LANES
    points = probe_store.shape[-1]
    modes = probe_store.shape[1]
    slot_count = amplitudes.shape[0]
    scan_count = owner.shape[0]
    channels = 2 * modes
    swaps = size == 16
    own_probe = probe_store.reshape(1, channels, points, points)

    is_live = (jnp.arange(slot_count, dtype=jnp.int32) < counts[0]).astype(jnp.int32)
    meta = jnp.stack([offsets[:, 0] - device * tile_rows, offsets[:, 1], scan_of, is_live], axis=1).reshape(-1)
    above = moved(meta, 1)

    if swaps:
        held = {0: own_probe}
        for far in (12, 8, 4):
            held[far] = swapped(own_probe, far)
        for far in (0, 12, 8, 4):
            held[far | 2] = swapped(held[far], 2)
        for far in (0, 2, 12, 14, 8, 10, 4, 6):
            held[far | 1] = swapped(held[far], 1)
        order = [far | side | core for core in (0, 1) for far in (12, 8, 4, 0) for side in (0, 2)]
        pieces = [held[k] for k in order]
        place = np.zeros(size, np.int32)
        place[np.array(order)] = np.arange(size)
        slot_of = jnp.asarray(place)[jnp.bitwise_xor(owner, device)]
        group_sizes = (2,) * 8
    else:
        owned = (owner == device)[:, None, None, None]
        pieces = [lax.psum(jnp.where(owned, own_probe, 0.0), "row")]
        slot_of = jnp.arange(scan_count, dtype=jnp.int32)
        group_sizes = (scan_count,)
    rim = moved(object_strip[:, :points, :], -1)

    num_top, num_low, squares, *groups = update(
        meta, slot_of, counts, amplitudes, object_strip, rim, transform_tables(points), pieces, group_sizes
    )

    if swaps:
        mine, theirs = groups[:4], groups[4:]
        other = [swapped(block, 1) for block in theirs]
        near = []
        for j in range(4):
            across = swapped(mine[j][1] + other[j][1], 2)
            near.append(mine[j][0] + other[j][0] + across)
        total = near[3]
        for j, far in enumerate((12, 8, 4)):
            total = total + swapped(near[j], far)
    else:
        summed = lax.psum(groups[0], "row")
        total = jnp.sum(jnp.where(owned, summed, 0.0), axis=0)
    received = moved(num_low, 1)
    density = density_of(meta, above, squares, tile_rows, blocks)
    new_object = finish(object_strip, num_top, received, density)
    new_probes = own_probe[0] + total[:channels] / (total[channels] + damping)
    return (new_object, new_probes.reshape(probe_store.shape))


def solution(mesh):
    return jax.shard_map(
        local,
        mesh=mesh,
        in_specs=(
            P(None, ("grp", "row"), None),
            P(("grp", "row"), None, None, None, None),
            P(("grp", "row"), None, None),
            P(("grp", "row")),
            P(("grp", "row"), None),
            P(("grp", "row")),
            P("grp"),
        ),
        out_specs=(P(None, ("grp", "row"), None), P(("grp", "row"), None, None, None, None)),
        check_vma=False,
    )
```

```python
import functools
import math

import jax
import jax.numpy as jnp
import numpy as np
from jax import lax
from jax.experimental import pallas as pl
from jax.experimental.pallas import tpu as pltpu
from jax.sharding import PartitionSpec as P

damping = 1.0
floor_level = 0.3
LANES = 128
SLOTS_AT_ONCE = 2
VMEM_BYTES = 48 * 1024 * 1024


def moved(block, distance):
    size = lax.axis_size("row")
    return lax.ppermute(block, "row", [(i, i + distance) for i in range(size) if 0 <= i + distance < size])


def swapped(block, mask):
    return lax.ppermute(block, "row", [(i, i ^ mask) for i in range(lax.axis_size("row"))])


FAR, NEAR = (8, 10, 14, 12), (0, 2, 6, 4)


def reduced(far, near):
    half = far[0].shape[2] // 2
    totals = []
    for part, (first, second) in enumerate(((2, 4), (4, 2))):
        rows = slice(part * half, (part + 1) * half)
        sent, kept = ((1, 2), (0, 3)) if first == 2 else ((3, 2), (0, 1))

        def pick(pair, at):
            return pair[0][at, :, rows] + pair[1][at, :, rows]

        def once(pair):
            got = swapped(jnp.stack([pick(pair, at) for at in sent]), first)
            return pick(pair, kept[0]) + got[0], pick(pair, kept[1]) + got[1]

        outer, across = once(far)
        inner, beside = once(near)
        outer = outer + swapped(across, second)
        totals.append(inner + swapped(beside, second) + swapped(outer, 8))
    return jnp.concatenate(totals, axis=1)


def split(value):
    high = value.astype(jnp.bfloat16)
    low = (value - high.astype(jnp.float32)).astype(jnp.bfloat16)
    return high, low


def transform_tables(points):
    index = np.arange(points)
    angle = (index[:, None] * index[None, :] % points) * (2.0 * math.pi / points)
    cos, sin = np.cos(angle) / math.sqrt(points), np.sin(angle) / math.sqrt(points)
    minus = np.block([[cos, -sin], [sin, cos]])
    plus = np.block([[cos, sin], [-sin, cos]])

    def parts(matrix, axis):
        matrix = matrix.astype(np.float32)
        high = matrix.astype(jnp.bfloat16)
        low = (matrix - high.astype(np.float32)).astype(jnp.bfloat16)
        return jnp.asarray(np.concatenate([high, high, low], axis=axis))

    return parts(minus, 0), parts(plus, 1), parts(minus, 1), parts(plus, 0)


def right_product(rows, table):
    high, low = split(rows)
    return jnp.dot(jnp.concatenate([high, low, high], axis=1), table, preferred_element_type=jnp.float32)


def left_product(table, columns):
    high, low = split(columns)
    return jnp.dot(table, jnp.concatenate([high, low, high], axis=0), preferred_element_type=jnp.float32)


def update_kernel(dims, meta, slot_of, live, amplitudes, obj, rim, *rest):
    piece_sizes, group_sizes, slots = dims
    tables = rest[:4]
    pieces = rest[4 : 4 + len(piece_sizes)]
    rest = rest[4 + len(piece_sizes) :]
    num_top, num_low, squares = rest[:3]
    groups = rest[3 : 3 + len(group_sizes)]
    table, ext, acc, part, right_f, left_f, left_i, right_i, piece_sems, out_sems = rest[3 + len(group_sizes) :]
    points = LANES
    tile_rows = obj.shape[1]
    blocks = obj.shape[2] // LANES
    modes = table.shape[1] // 2

    copies = []
    at = 0
    for k, size in enumerate(piece_sizes):
        copies.append(pltpu.make_async_copy(pieces[k], table.at[pl.ds(at, size)], piece_sems.at[k]))
        at += size
    for k, (source, target) in enumerate(zip(tables, (right_f, left_f, left_i, right_i))):
        copies.append(pltpu.make_async_copy(source, target, piece_sems.at[len(piece_sizes) + k]))
    for copy in copies:
        copy.start()
    for b in range(blocks):
        ext[:, b, :tile_rows, :] = obj[:, :, b * LANES : (b + 1) * LANES]
        ext[:, b, tile_rows:, :] = rim[:, :, b * LANES : (b + 1) * LANES]
    ext[:, blocks] = jnp.zeros_like(ext[:, blocks])
    acc[...] = jnp.zeros_like(acc)
    part[...] = jnp.zeros_like(part)
    for copy in copies:
        copy.wait()
    for s in range(squares.shape[0]):
        probe = table[slot_of[s]]
        squares[s] = jnp.sum(probe * probe, axis=0)

    lane = lax.broadcasted_iota(jnp.int32, (points, LANES), 1)
    count = live[0]

    def step(i, carry):
        wins, probes, places, waves, flags = [], [], [], [], []
        for u in range(SLOTS_AT_ONCE):
            p = i * SLOTS_AT_ONCE + u
            flags.append((p < count).astype(jnp.float32))
            row, col, scan = meta[4 * p], meta[4 * p + 1], meta[4 * p + 2]
            slot = slot_of[scan]
            block, shift = col // LANES, col % LANES
            back = lax.rem(LANES - shift, LANES)
            keep = lane < LANES - shift
            win = []
            for ch in range(2):
                first = pltpu.roll(ext[ch, block, pl.ds(row, points), :], back, 1)
                second = pltpu.roll(ext[ch, block + 1, pl.ds(row, points), :], back, 1)
                win.append(jnp.where(keep, first, second))
            probe = [(table[slot, 2 * m], table[slot, 2 * m + 1]) for m in range(modes)]
            for pr, pi in probe:
                waves.append(
                    jnp.concatenate([pr * win[0] - pi * win[1], pr * win[1] + pi * win[0]], axis=1)
                )
            wins.append(win)
            probes.append(probe)
            places.append((p, row, block, shift, slot))
        half = right_product(jnp.concatenate(waves, axis=0), right_f[...])
        columns = []
        for k in range(SLOTS_AT_ONCE * modes):
            rows = half[k * points : (k + 1) * points]
            columns.append(jnp.concatenate([rows[:, :points], rows[:, points:]], axis=0))
        spec = left_product(left_f[...], jnp.concatenate(columns, axis=1))
        columns = []
        for u in range(SLOTS_AT_ONCE):
            own = [spec[:, (u * modes + m) * points : (u * modes + m + 1) * points] for m in range(modes)]
            total = functools.reduce(jnp.add, [s * s for s in own])
            intensity = total[:points] + total[points:]
            factor = amplitudes[places[u][0]] * lax.rsqrt(jnp.maximum(intensity, floor_level * floor_level)) - 1.0
            factor = factor * flags[u]
            factor = jnp.concatenate([factor, factor], axis=0)
            columns += [s * factor for s in own]
        half = left_product(left_i[...], jnp.concatenate(columns, axis=1))
        rows = []
        for k in range(SLOTS_AT_ONCE * modes):
            column = half[:, k * points : (k + 1) * points]
            rows.append(jnp.concatenate([column[:points], column[points:]], axis=1))
        change = right_product(jnp.concatenate(rows, axis=0), right_i[...])
        for u in range(SLOTS_AT_ONCE):
            p, row, block, shift, slot = places[u]
            wr, wi = wins[u]
            term_r = term_i = None
            for m in range(modes):
                k = u * modes + m
                pr, pi = probes[u][m]
                dr = change[k * points : (k + 1) * points, :points]
                di = change[k * points : (k + 1) * points, points:]
                tr, ti = pr * dr + pi * di, pr * di - pi * dr
                term_r = tr if m == 0 else term_r + tr
                term_i = ti if m == 0 else term_i + ti
                part[slot, 2 * m] += wr * dr + wi * di
                part[slot, 2 * m + 1] += wr * di - wi * dr
            part[slot, 2 * modes] += (wr * wr + wi * wi) * flags[u]
            first = lane >= shift
            for ch, term in enumerate((term_r, term_i)):
                term = pltpu.roll(term, shift, 1)
                acc[ch, block, pl.ds(row, points), :] += jnp.where(first, term, 0.0)
                acc[ch, block + 1, pl.ds(row, points), :] += jnp.where(first, 0.0, term)
        return carry

    lax.fori_loop(0, (count + SLOTS_AT_ONCE - 1) // SLOTS_AT_ONCE, step, 0)

    copies = []
    at = 0
    for k, size in enumerate(group_sizes):
        copies.append(pltpu.make_async_copy(part.at[pl.ds(at, size)], groups[k], out_sems.at[k]))
        at += size
    k = len(group_sizes)
    copies.append(
        pltpu.make_async_copy(acc.at[:, pl.ds(0, blocks), pl.ds(tile_rows, points), :], num_low, out_sems.at[k])
    )
    copies.append(
        pltpu.make_async_copy(acc.at[:, pl.ds(0, blocks), pl.ds(0, tile_rows), :], num_top, out_sems.at[k + 1])
    )
    for copy in copies:
        copy.start()
    for copy in copies:
        copy.wait()


def update(meta, slot_of, live, amplitudes, obj, rim, tables, pieces, group_sizes):
    points = amplitudes.shape[-1]
    tile_rows = obj.shape[1]
    blocks = obj.shape[2] // LANES
    channels = pieces[0].shape[1]
    scans = slot_of.shape[0]
    piece_sizes = tuple(piece.shape[0] for piece in pieces)
    slots = sum(piece_sizes)
    f32 = jnp.float32
    smem = pl.BlockSpec(memory_space=pltpu.SMEM)
    vmem = pl.BlockSpec(memory_space=pltpu.VMEM)
    anywhere = pl.BlockSpec(memory_space=pl.ANY)
    return pl.pallas_call(
        functools.partial(update_kernel, (piece_sizes, group_sizes, slots)),
        out_shape=[
            jax.ShapeDtypeStruct((2, blocks, tile_rows, LANES), f32),
            jax.ShapeDtypeStruct((2, blocks, points, LANES), f32),
            jax.ShapeDtypeStruct((scans, points, points), f32),
        ]
        + [jax.ShapeDtypeStruct((size, channels + 1, points, points), f32) for size in group_sizes],
        in_specs=[smem] * 3 + [vmem] * 3 + [anywhere] * (4 + len(pieces)),
        out_specs=[anywhere, anywhere, vmem] + [anywhere] * len(group_sizes),
        scratch_shapes=[
            pltpu.VMEM((slots, channels, points, points), f32),
            pltpu.VMEM((2, blocks + 1, tile_rows + points, LANES), f32),
            pltpu.VMEM((2, blocks + 1, tile_rows + points, LANES), f32),
            pltpu.VMEM((slots, channels + 1, points, points), f32),
        ]
        + [pltpu.VMEM(factor.shape, factor.dtype) for factor in tables]
        + [
            pltpu.SemaphoreType.DMA((len(pieces) + 4,)),
            pltpu.SemaphoreType.DMA((len(group_sizes) + 2,)),
        ],
        compiler_params=pltpu.CompilerParams(vmem_limit_bytes=VMEM_BYTES),
        cost_estimate=pl.CostEstimate(flops=6 * 10**9, bytes_accessed=16 * 2**20, transcendentals=2**18),
        name="update",
    )(meta, slot_of, live, amplitudes, obj, rim, *tables, *pieces)


def density_kernel(tile_rows, meta, above, squares, density, ext):
    points = LANES
    blocks = density.shape[0]
    ext[...] = jnp.zeros_like(ext)
    lane = lax.broadcasted_iota(jnp.int32, (points, LANES), 1)

    def place(values, row, col):
        block, shift = col // LANES, col % LANES
        first = lane >= shift
        values = pltpu.roll(values, shift, 1)
        ext[block, pl.ds(row, points), :] += jnp.where(first, values, 0.0)
        ext[block + 1, pl.ds(row, points), :] += jnp.where(first, 0.0, values)

    def own(p, carry):
        @pl.when(meta[4 * p + 3] > 0)
        def _():
            place(squares[meta[4 * p + 2]], meta[4 * p] + points, meta[4 * p + 1])

        return carry

    def upper(p, carry):
        row = above[4 * p] - tile_rows + points

        @pl.when((above[4 * p + 3] > 0) & (row > 0))
        def _():
            place(squares[above[4 * p + 2]], row, above[4 * p + 1])

        return carry

    lax.fori_loop(0, meta.shape[0] // 4, own, 0)
    lax.fori_loop(0, above.shape[0] // 4, upper, 0)
    density[...] = ext[:blocks, points : points + tile_rows, :]


def density_of(meta, above, squares, tile_rows, blocks):
    points = squares.shape[-1]
    smem = pl.BlockSpec(memory_space=pltpu.SMEM)
    vmem = pl.BlockSpec(memory_space=pltpu.VMEM)
    return pl.pallas_call(
        functools.partial(density_kernel, tile_rows),
        out_shape=jax.ShapeDtypeStruct((blocks, tile_rows, LANES), jnp.float32),
        in_specs=[smem, smem, vmem],
        out_specs=vmem,
        scratch_shapes=[pltpu.VMEM((blocks + 1, points + tile_rows + points, LANES), jnp.float32)],
        compiler_params=pltpu.CompilerParams(vmem_limit_bytes=VMEM_BYTES),
        cost_estimate=pl.CostEstimate(flops=2**23, bytes_accessed=8 * 2**20, transcendentals=0),
        name="density",
    )(meta, above, squares)


def finish_kernel(obj, num_top, received, density, out):
    points = received.shape[2]
    for b in range(density.shape[0]):
        columns = slice(b * LANES, (b + 1) * LANES)
        scale = 1.0 / (density[b] + damping)
        for ch in range(2):
            head = num_top[ch, b, :points] + received[ch, b]
            out[ch, :points, columns] = obj[ch, :points, columns] + head * scale[:points]
            out[ch, points:, columns] = obj[ch, points:, columns] + num_top[ch, b, points:] * scale[points:]


def finish(obj, num_top, received, density):
    vmem = pl.BlockSpec(memory_space=pltpu.VMEM)
    return pl.pallas_call(
        finish_kernel,
        out_shape=jax.ShapeDtypeStruct(obj.shape, obj.dtype),
        in_specs=[vmem] * 4,
        out_specs=vmem,
        compiler_params=pltpu.CompilerParams(vmem_limit_bytes=VMEM_BYTES),
        cost_estimate=pl.CostEstimate(flops=2**21, bytes_accessed=8 * 2**20, transcendentals=0),
        name="finish",
    )(obj, num_top, received, density)


def local(object_strip, probe_store, amplitudes, scan_of, offsets, counts, owner):
    device = lax.axis_index("row")
    size = lax.axis_size("row")
    tile_rows = object_strip.shape[1]
    blocks = object_strip.shape[2] // LANES
    points = probe_store.shape[-1]
    modes = probe_store.shape[1]
    slot_count = amplitudes.shape[0]
    scan_count = owner.shape[0]
    channels = 2 * modes
    swaps = size == 16
    own_probe = probe_store.reshape(1, channels, points, points)

    is_live = (jnp.arange(slot_count, dtype=jnp.int32) < counts[0]).astype(jnp.int32)
    meta = jnp.stack([offsets[:, 0] - device * tile_rows, offsets[:, 1], scan_of, is_live], axis=1).reshape(-1)
    above = moved(meta, 1)

    if swaps:
        held = {0: own_probe}
        for key in (8, 4, 2):
            held[key] = swapped(own_probe, key)
        held[6] = swapped(held[4], 2)
        held[12] = swapped(held[8], 4)
        held[10] = swapped(held[8], 2)
        held[14] = swapped(held[12], 2)
        for key in list(held):
            held[key | 1] = swapped(held[key], 1)
        order = [key | core for core in (0, 1) for key in FAR + NEAR]
        pieces = [held[key] for key in order]
        place = np.zeros(size, np.int32)
        place[np.array(order)] = np.arange(size)
        slot_of = jnp.asarray(place)[jnp.bitwise_xor(owner, device)]
        group_sizes = (4,) * 4
    else:
        owned = (owner == device)[:, None, None, None]
        pieces = [lax.psum(jnp.where(owned, own_probe, 0.0), "row")]
        slot_of = jnp.arange(scan_count, dtype=jnp.int32)
        group_sizes = (scan_count,)
    rim = moved(object_strip[:, :points, :], -1)

    num_top, num_low, squares, *groups = update(
        meta, slot_of, counts, amplitudes, object_strip, rim, transform_tables(points), pieces, group_sizes
    )

    received = moved(num_low, 1)
    if swaps:
        mine_far, mine_near, theirs_far, theirs_near = groups
        total = reduced((mine_far, swapped(theirs_far, 1)), (mine_near, swapped(theirs_near, 1)))
    else:
        summed = lax.psum(groups[0], "row")
        total = jnp.sum(jnp.where(owned, summed, 0.0), axis=0)
    density = density_of(meta, above, squares, tile_rows, blocks)
    new_object = finish(object_strip, num_top, received, density)
    new_probes = own_probe[0] + total[:channels] / (total[channels] + damping)
    return (new_object, new_probes.reshape(probe_store.shape))


def solution(mesh):
    return jax.shard_map(
        local,
        mesh=mesh,
        in_specs=(
            P(None, ("grp", "row"), None),
            P(("grp", "row"), None, None, None, None),
            P(("grp", "row"), None, None),
            P(("grp", "row")),
            P(("grp", "row"), None),
            P(("grp", "row")),
            P("grp"),
        ),
        out_specs=(P(None, ("grp", "row"), None), P(("grp", "row"), None, None, None, None)),
        check_vma=False,
    )
```

```python
import functools
import math

import jax
import jax.numpy as jnp
import numpy as np
from jax import lax
from jax.experimental import pallas as pl
from jax.experimental.pallas import tpu as pltpu
from jax.sharding import PartitionSpec as P

damping = 1.0
floor_level = 0.3
LANES = 128
SLOTS_AT_ONCE = 4
VMEM_BYTES = 48 * 1024 * 1024


def moved(block, distance):
    size = lax.axis_size("row")
    return lax.ppermute(block, "row", [(i, i + distance) for i in range(size) if 0 <= i + distance < size])


def swapped(block, mask):
    return lax.ppermute(block, "row", [(i, i ^ mask) for i in range(lax.axis_size("row"))])


FAR, NEAR = (8, 10, 14, 12), (0, 2, 6, 4)


def reduced(far, theirs_near, mine_near, low, density):
    half = far[0].shape[2] // 2
    routes = ((slice(0, half), 2, 4, (1, 2), 3), (slice(half, 2 * half), 4, 2, (3, 2), 1))

    def pick(pair, at, rows):
        return pair[0][at, :, rows] + pair[1][at, :, rows]

    def first_step(pair):
        return [swapped(jnp.stack([pick(pair, at, rows) for at in sent]), mask) for rows, mask, _, sent, _ in routes]

    got = first_step(far)
    near = (mine_near, swapped(theirs_near, 1))
    got_near = first_step(near)
    low = after(low, *got)
    received = moved(low, 1)
    outer, across = [], []
    for (rows, _, second, _, kept), arrived in zip(routes, got):
        outer.append(pick(far, 0, rows) + arrived[0])
        across.append(pick(far, kept, rows) + arrived[1])
    density, across[0] = lax.optimization_barrier((density, across[0]))
    across = [swapped(block, route[2]) for block, route in zip(across, routes)]
    beside = []
    for (rows, _, second, _, kept), arrived in zip(routes, got_near):
        beside.append(swapped(pick(near, kept, rows) + arrived[1], second))
    totals = []
    for k, (rows, _, _, _, _) in enumerate(routes):
        ahead = swapped(outer[k] + across[k], 8)
        totals.append(pick(near, 0, rows) + got_near[k][0] + beside[k] + ahead)
    return jnp.concatenate(totals, axis=1), received, density


def after(value, *others):
    return lax.optimization_barrier((value,) + others)[0]


def split(value):
    high = value.astype(jnp.bfloat16)
    low = (value - high.astype(jnp.float32)).astype(jnp.bfloat16)
    return high, low


def transform_tables(points):
    index = np.arange(points)
    angle = (index[:, None] * index[None, :] % points) * (2.0 * math.pi / points)
    cos, sin = np.cos(angle) / math.sqrt(points), np.sin(angle) / math.sqrt(points)
    minus = np.block([[cos, -sin], [sin, cos]])
    plus = np.block([[cos, sin], [-sin, cos]])

    parts = []
    for matrix in (minus.astype(np.float32), plus.astype(np.float32)):
        high = matrix.astype(jnp.bfloat16)
        parts += [high, (matrix - high.astype(np.float32)).astype(jnp.bfloat16)]
    return jnp.asarray(np.stack(parts))


def right_product(rows, factor, at):
    high, low = split(rows)
    table = jnp.concatenate([factor[at], factor[at], factor[at + 1]], axis=0)
    return jnp.dot(jnp.concatenate([high, low, high], axis=1), table, preferred_element_type=jnp.float32)


def left_product(factor, at, columns):
    high, low = split(columns)
    table = jnp.concatenate([factor[at], factor[at], factor[at + 1]], axis=1)
    return jnp.dot(table, jnp.concatenate([high, low, high], axis=0), preferred_element_type=jnp.float32)


def update_kernel(dims, meta, slot_of, live, amplitudes_in, obj, rim, factors_in, *rest):
    piece_sizes, group_sizes, slots = dims
    pieces = rest[: len(piece_sizes)]
    rest = rest[len(piece_sizes) :]
    num_top, num_low, squares = rest[:3]
    groups = rest[3 : 3 + len(group_sizes)]
    table, ext, acc, part, amplitudes, factors, in_sems, out_sems = rest[3 + len(group_sizes) :]
    points = LANES
    tile_rows = obj.shape[1]
    blocks = obj.shape[2] // LANES
    modes = table.shape[1] // 2

    moves = [(factors_in, factors), (amplitudes_in, amplitudes)]
    for b in range(blocks):
        columns = pl.ds(b * LANES, LANES)
        moves.append((obj.at[:, :, columns], ext.at[:, b, pl.ds(0, tile_rows), :]))
        moves.append((rim.at[:, :, columns], ext.at[:, b, pl.ds(tile_rows, points), :]))
    at = 0
    for k, size in enumerate(piece_sizes):
        moves.append((pieces[k], table.at[pl.ds(at, size)]))
        at += size
    copies = [pltpu.make_async_copy(*ends, in_sems.at[k]) for k, ends in enumerate(moves)]
    for copy in copies:
        copy.start()
    acc[...] = jnp.zeros_like(acc)
    part[...] = jnp.zeros_like(part)
    for copy in copies:
        copy.wait()
    for s in range(squares.shape[0]):
        probe = table[slot_of[s]]
        squares[s] = jnp.sum(probe * probe, axis=0)

    lane = lax.broadcasted_iota(jnp.int32, (points, LANES), 1)
    count = live[0]

    def step(i, carry):
        wins, probes, places, waves, flags = [], [], [], [], []
        for u in range(SLOTS_AT_ONCE):
            p = i * SLOTS_AT_ONCE + u
            flags.append((p < count).astype(jnp.float32))
            row, col, scan = meta[4 * p], meta[4 * p + 1], meta[4 * p + 2]
            slot = slot_of[scan]
            block, shift = col // LANES, col % LANES
            back = lax.rem(LANES - shift, LANES)
            keep = lane >= shift
            win = []
            for ch in range(2):
                first = ext[ch, block, pl.ds(row, points), :]
                second = ext[ch, block + 1, pl.ds(row, points), :]
                win.append(pltpu.roll(jnp.where(keep, first, second), back, 1))
            probe = [(table[slot, 2 * m], table[slot, 2 * m + 1]) for m in range(modes)]
            for pr, pi in probe:
                waves.append(
                    jnp.concatenate([pr * win[0] - pi * win[1], pr * win[1] + pi * win[0]], axis=1)
                )
            wins.append(win)
            probes.append(probe)
            places.append((p, row, block, shift, slot))
        half = right_product(jnp.concatenate(waves, axis=0), factors, 0)
        columns = []
        for k in range(SLOTS_AT_ONCE * modes):
            rows = half[k * points : (k + 1) * points]
            columns.append(jnp.concatenate([rows[:, :points], rows[:, points:]], axis=0))
        spec = left_product(factors, 2, jnp.concatenate(columns, axis=1))
        columns = []
        for u in range(SLOTS_AT_ONCE):
            own = [spec[:, (u * modes + m) * points : (u * modes + m + 1) * points] for m in range(modes)]
            total = functools.reduce(jnp.add, [s * s for s in own])
            intensity = total[:points] + total[points:]
            factor = amplitudes[places[u][0]] * lax.rsqrt(jnp.maximum(intensity, floor_level * floor_level)) - 1.0
            factor = factor * flags[u]
            factor = jnp.concatenate([factor, factor], axis=0)
            columns += [s * factor for s in own]
        half = left_product(factors, 0, jnp.concatenate(columns, axis=1))
        rows = []
        for k in range(SLOTS_AT_ONCE * modes):
            column = half[:, k * points : (k + 1) * points]
            rows.append(jnp.concatenate([column[:points], column[points:]], axis=1))
        change = right_product(jnp.concatenate(rows, axis=0), factors, 2)
        for u in range(SLOTS_AT_ONCE):
            p, row, block, shift, slot = places[u]
            wr, wi = wins[u]
            term_r = term_i = None
            for m in range(modes):
                k = u * modes + m
                pr, pi = probes[u][m]
                dr = change[k * points : (k + 1) * points, :points]
                di = change[k * points : (k + 1) * points, points:]
                tr, ti = pr * dr + pi * di, pr * di - pi * dr
                term_r = tr if m == 0 else term_r + tr
                term_i = ti if m == 0 else term_i + ti
                part[slot, 2 * m] += wr * dr + wi * di
                part[slot, 2 * m + 1] += wr * di - wi * dr
            part[slot, 2 * modes] += (wr * wr + wi * wi) * flags[u]
            first = lane >= shift
            for ch, term in enumerate((term_r, term_i)):
                term = pltpu.roll(term, shift, 1)
                acc[ch, block, pl.ds(row, points), :] += jnp.where(first, term, 0.0)
                acc[ch, block + 1, pl.ds(row, points), :] += jnp.where(first, 0.0, term)
        return carry

    lax.fori_loop(0, (count + SLOTS_AT_ONCE - 1) // SLOTS_AT_ONCE, step, 0)

    copies = []
    at = 0
    for k, size in enumerate(group_sizes):
        copies.append(pltpu.make_async_copy(part.at[pl.ds(at, size)], groups[k], out_sems.at[k]))
        at += size
    k = len(group_sizes)
    copies.append(
        pltpu.make_async_copy(acc.at[:, pl.ds(0, blocks), pl.ds(tile_rows, points), :], num_low, out_sems.at[k])
    )
    copies.append(
        pltpu.make_async_copy(acc.at[:, pl.ds(0, blocks), pl.ds(0, tile_rows), :], num_top, out_sems.at[k + 1])
    )
    for copy in copies:
        copy.start()
    for copy in copies:
        copy.wait()


def update(meta, slot_of, live, amplitudes, obj, rim, factors, pieces, group_sizes):
    points = amplitudes.shape[-1]
    tile_rows = obj.shape[1]
    blocks = obj.shape[2] // LANES
    channels = pieces[0].shape[1]
    scans = slot_of.shape[0]
    piece_sizes = tuple(piece.shape[0] for piece in pieces)
    slots = sum(piece_sizes)
    f32 = jnp.float32
    smem = pl.BlockSpec(memory_space=pltpu.SMEM)
    vmem = pl.BlockSpec(memory_space=pltpu.VMEM)
    anywhere = pl.BlockSpec(memory_space=pl.ANY)
    return pl.pallas_call(
        functools.partial(update_kernel, (piece_sizes, group_sizes, slots)),
        out_shape=[
            jax.ShapeDtypeStruct((2, blocks, tile_rows, LANES), f32),
            jax.ShapeDtypeStruct((2, blocks, points, LANES), f32),
            jax.ShapeDtypeStruct((scans, points, points), f32),
        ]
        + [jax.ShapeDtypeStruct((size, channels + 1, points, points), f32) for size in group_sizes],
        in_specs=[smem] * 3 + [anywhere] * 3 + [pl.BlockSpec(memory_space=pltpu.HBM)] + [anywhere] * len(pieces),
        out_specs=[anywhere, anywhere, vmem] + [anywhere] * len(group_sizes),
        scratch_shapes=[
            pltpu.VMEM((slots, channels, points, points), f32),
            pltpu.VMEM((2, blocks + 1, tile_rows + points, LANES), f32),
            pltpu.VMEM((2, blocks + 1, tile_rows + points, LANES), f32),
            pltpu.VMEM((slots, channels + 1, points, points), f32),
            pltpu.VMEM(amplitudes.shape, f32),
            pltpu.VMEM(factors.shape, factors.dtype),
            pltpu.SemaphoreType.DMA((len(pieces) + 2 * blocks + 2,)),
            pltpu.SemaphoreType.DMA((len(group_sizes) + 2,)),
        ],
        compiler_params=pltpu.CompilerParams(vmem_limit_bytes=VMEM_BYTES),
        cost_estimate=pl.CostEstimate(flops=6 * 10**9, bytes_accessed=16 * 2**20, transcendentals=2**18),
        name="update",
    )(meta, slot_of, live, amplitudes, obj, rim, factors, *pieces)


def density_kernel(tile_rows, meta, above, squares, density, ext):
    points = LANES
    blocks = density.shape[0]
    ext[...] = jnp.zeros_like(ext)
    lane = lax.broadcasted_iota(jnp.int32, (points, LANES), 1)

    def place(values, row, col):
        block, shift = col // LANES, col % LANES
        first = lane >= shift
        values = pltpu.roll(values, shift, 1)
        ext[block, pl.ds(row, points), :] += jnp.where(first, values, 0.0)
        ext[block + 1, pl.ds(row, points), :] += jnp.where(first, 0.0, values)

    def own(p, carry):
        @pl.when(meta[4 * p + 3] > 0)
        def _():
            place(squares[meta[4 * p + 2]], meta[4 * p] + points, meta[4 * p + 1])

        return carry

    def upper(p, carry):
        row = above[4 * p] - tile_rows + points

        @pl.when((above[4 * p + 3] > 0) & (row > 0))
        def _():
            place(squares[above[4 * p + 2]], row, above[4 * p + 1])

        return carry

    lax.fori_loop(0, meta.shape[0] // 4, own, 0)
    lax.fori_loop(0, above.shape[0] // 4, upper, 0)
    density[...] = ext[:blocks, points : points + tile_rows, :]


def density_of(meta, above, squares, tile_rows, blocks):
    points = squares.shape[-1]
    smem = pl.BlockSpec(memory_space=pltpu.SMEM)
    vmem = pl.BlockSpec(memory_space=pltpu.VMEM)
    return pl.pallas_call(
        functools.partial(density_kernel, tile_rows),
        out_shape=jax.ShapeDtypeStruct((blocks, tile_rows, LANES), jnp.float32),
        in_specs=[smem, smem, vmem],
        out_specs=vmem,
        scratch_shapes=[pltpu.VMEM((blocks + 1, points + tile_rows + points, LANES), jnp.float32)],
        compiler_params=pltpu.CompilerParams(vmem_limit_bytes=VMEM_BYTES),
        cost_estimate=pl.CostEstimate(flops=2**23, bytes_accessed=8 * 2**20, transcendentals=0),
        name="density",
    )(meta, above, squares)


def finish_kernel(obj, num_top, received, density, out):
    points = received.shape[2]
    for b in range(density.shape[0]):
        columns = slice(b * LANES, (b + 1) * LANES)
        scale = 1.0 / (density[b] + damping)
        for ch in range(2):
            head = num_top[ch, b, :points] + received[ch, b]
            out[ch, :points, columns] = obj[ch, :points, columns] + head * scale[:points]
            out[ch, points:, columns] = obj[ch, points:, columns] + num_top[ch, b, points:] * scale[points:]


def finish(obj, num_top, received, density):
    vmem = pl.BlockSpec(memory_space=pltpu.VMEM)
    return pl.pallas_call(
        finish_kernel,
        out_shape=jax.ShapeDtypeStruct(obj.shape, obj.dtype),
        in_specs=[vmem] * 4,
        out_specs=vmem,
        compiler_params=pltpu.CompilerParams(vmem_limit_bytes=VMEM_BYTES),
        cost_estimate=pl.CostEstimate(flops=2**21, bytes_accessed=8 * 2**20, transcendentals=0),
        name="finish",
    )(obj, num_top, received, density)


def local(object_strip, probe_store, amplitudes, scan_of, offsets, counts, owner):
    device = lax.axis_index("row")
    size = lax.axis_size("row")
    tile_rows = object_strip.shape[1]
    blocks = object_strip.shape[2] // LANES
    points = probe_store.shape[-1]
    modes = probe_store.shape[1]
    slot_count = amplitudes.shape[0]
    scan_count = owner.shape[0]
    channels = 2 * modes
    swaps = size == 16
    own_probe = probe_store.reshape(1, channels, points, points)

    is_live = (jnp.arange(slot_count, dtype=jnp.int32) < counts[0]).astype(jnp.int32)
    meta = jnp.stack([offsets[:, 0] - device * tile_rows, offsets[:, 1], scan_of, is_live], axis=1).reshape(-1)
    above = moved(meta, 1)

    if swaps:
        held = {0: own_probe}
        for key in (8, 4, 2):
            held[key] = swapped(own_probe, key)
        held[6] = swapped(held[4], 2)
        held[12] = swapped(held[8], 4)
        held[10] = swapped(held[8], 2)
        held[14] = swapped(held[12], 2)
        held[10] = after(held[10], above)
        for key in list(held):
            held[key | 1] = swapped(held[key], 1)
        order = [key | core for core in (0, 1) for key in FAR + NEAR]
        pieces = [held[key] for key in order]
        key = jnp.bitwise_xor(owner, device)
        side = key // 2 % 4
        slot_of = key % 2 * 8 + (1 - key // 8) * 4 + jnp.bitwise_xor(side, side // 2)
        group_sizes = (4,) * 4
    else:
        owned = (owner == device)[:, None, None, None]
        pieces = [lax.psum(jnp.where(owned, own_probe, 0.0), "row")]
        slot_of = jnp.arange(scan_count, dtype=jnp.int32)
        group_sizes = (scan_count,)
    rim = moved(object_strip[:, :points, :], -1)

    num_top, num_low, squares, *groups = update(
        meta, slot_of, counts, amplitudes, object_strip, rim, transform_tables(points), pieces, group_sizes
    )

    density = density_of(meta, above, squares, tile_rows, blocks)
    if swaps:
        mine_far, mine_near, theirs_far, theirs_near = groups
        total, received, density = reduced((mine_far, swapped(theirs_far, 1)), theirs_near, mine_near, num_low, density)
    else:
        received = moved(num_low, 1)
        summed = lax.psum(groups[0], "row")
        total = jnp.sum(jnp.where(owned, summed, 0.0), axis=0)
    new_object = finish(object_strip, num_top, received, density)
    new_probes = own_probe[0] + total[:channels] / (total[channels] + damping)
    return (new_object, new_probes.reshape(probe_store.shape))


def solution(mesh):
    return jax.shard_map(
        local,
        mesh=mesh,
        in_specs=(
            P(None, ("grp", "row"), None),
            P(("grp", "row"), None, None, None, None),
            P(("grp", "row"), None, None),
            P(("grp", "row")),
            P(("grp", "row"), None),
            P(("grp", "row")),
            P("grp"),
        ),
        out_specs=(P(None, ("grp", "row"), None), P(("grp", "row"), None, None, None, None)),
        check_vma=False,
    )
```

```python
import functools
import math

import jax
import jax.numpy as jnp
import numpy as np
from jax import lax
from jax.experimental import pallas as pl
from jax.experimental.pallas import tpu as pltpu
from jax.sharding import PartitionSpec as P

damping = 1.0
floor_level = 0.3
LANES = 128
SLOTS_AT_ONCE = 4
VMEM_BYTES = 26 * 1024 * 1024


def moved(block, distance):
    size = lax.axis_size("row")
    return lax.ppermute(block, "row", [(i, i + distance) for i in range(size) if 0 <= i + distance < size])


def swapped(block, mask):
    return lax.ppermute(block, "row", [(i, i ^ mask) for i in range(lax.axis_size("row"))])


FAR, NEAR = (8, 10, 14, 12), (0, 2, 6, 4)


def reduced(far, theirs_near, mine_near, low, density):
    half = far[0].shape[2] // 2
    routes = ((slice(0, half), 2, 4, (1, 2), 3), (slice(half, 2 * half), 4, 2, (3, 2), 1))

    def pick(pair, at, rows):
        return pair[0][at, :, rows] + pair[1][at, :, rows]

    def first_step(pair):
        return [swapped(jnp.stack([pick(pair, at, rows) for at in sent]), mask) for rows, mask, _, sent, _ in routes]

    got = first_step(far)
    near = (mine_near, swapped(theirs_near, 1))
    got_near = first_step(near)
    low = after(low, *got)
    received = moved(low, 1)
    outer, across = [], []
    for (rows, _, second, _, kept), arrived in zip(routes, got):
        outer.append(pick(far, 0, rows) + arrived[0])
        across.append(pick(far, kept, rows) + arrived[1])
    density, across[0] = lax.optimization_barrier((density, across[0]))
    across = [swapped(block, route[2]) for block, route in zip(across, routes)]
    beside = []
    for (rows, _, second, _, kept), arrived in zip(routes, got_near):
        beside.append(swapped(pick(near, kept, rows) + arrived[1], second))
    totals = []
    for k, (rows, _, _, _, _) in enumerate(routes):
        ahead = swapped(outer[k] + across[k], 8)
        totals.append(pick(near, 0, rows) + got_near[k][0] + beside[k] + ahead)
    return jnp.concatenate(totals, axis=1), received, density


def after(value, *others):
    return lax.optimization_barrier((value,) + others)[0]


def split(value):
    high = value.astype(jnp.bfloat16)
    low = (value - high.astype(jnp.float32)).astype(jnp.bfloat16)
    return high, low


def transform_tables(points):
    index = np.arange(points)
    angle = (index[:, None] * index[None, :] % points) * (2.0 * math.pi / points)
    cos, sin = np.cos(angle) / math.sqrt(points), np.sin(angle) / math.sqrt(points)
    minus = np.block([[cos, -sin], [sin, cos]])
    plus = np.block([[cos, sin], [-sin, cos]])

    parts = []
    for matrix in (minus.astype(np.float32), plus.astype(np.float32)):
        high = matrix.astype(jnp.bfloat16)
        parts += [high, (matrix - high.astype(np.float32)).astype(jnp.bfloat16)]
    return jnp.asarray(np.stack(parts))


def right_product(rows, factor, at):
    high, low = split(rows)
    table = jnp.concatenate([factor[at], factor[at], factor[at + 1]], axis=0)
    return jnp.dot(jnp.concatenate([high, low, high], axis=1), table, preferred_element_type=jnp.float32)


def left_product(factor, at, columns):
    high, low = split(columns)
    table = jnp.concatenate([factor[at], factor[at], factor[at + 1]], axis=1)
    return jnp.dot(table, jnp.concatenate([high, low, high], axis=0), preferred_element_type=jnp.float32)


def update_kernel(dims, meta, slot_of, live, amplitudes, obj, rim, factors, *rest):
    piece_sizes, group_sizes, slots = dims
    pieces = rest[: len(piece_sizes)]
    rest = rest[len(piece_sizes) :]
    num_top, num_low, squares = rest[:3]
    groups = rest[3 : 3 + len(group_sizes)]
    table, ext, acc, part, in_sems, out_sems = rest[3 + len(group_sizes) :]
    points = LANES
    tile_rows = obj.shape[1]
    blocks = obj.shape[2] // LANES
    modes = table.shape[1] // 2

    moves = []
    for b in range(blocks):
        columns = pl.ds(b * LANES, LANES)
        moves.append((obj.at[:, :, columns], ext.at[:, b, pl.ds(0, tile_rows), :]))
        moves.append((rim.at[:, :, columns], ext.at[:, b, pl.ds(tile_rows, points), :]))
    at = 0
    for k, size in enumerate(piece_sizes):
        moves.append((pieces[k], table.at[pl.ds(at, size)]))
        at += size
    copies = [pltpu.make_async_copy(*ends, in_sems.at[k]) for k, ends in enumerate(moves)]
    for copy in copies:
        copy.start()
    acc[...] = jnp.zeros_like(acc)
    part[...] = jnp.zeros_like(part)
    for copy in copies:
        copy.wait()
    for s in range(squares.shape[0]):
        probe = table[slot_of[s]]
        squares[s] = jnp.sum(probe * probe, axis=0)

    lane = lax.broadcasted_iota(jnp.int32, (points, LANES), 1)
    count = live[0]

    def step(i, carry):
        wins, probes, places, waves, flags = [], [], [], [], []
        for u in range(SLOTS_AT_ONCE):
            at = i * SLOTS_AT_ONCE + u
            flags.append((at < count).astype(jnp.float32))
            p = jnp.minimum(at, count - 1)
            row, col, scan = meta[4 * p], meta[4 * p + 1], meta[4 * p + 2]
            slot = slot_of[scan]
            block, shift = col // LANES, col % LANES
            back = lax.rem(LANES - shift, LANES)
            keep = lane >= shift
            win = []
            for ch in range(2):
                first = ext[ch, block, pl.ds(row, points), :]
                second = ext[ch, block + 1, pl.ds(row, points), :]
                win.append(pltpu.roll(jnp.where(keep, first, second), back, 1))
            probe = [(table[slot, 2 * m], table[slot, 2 * m + 1]) for m in range(modes)]
            for pr, pi in probe:
                waves.append(
                    jnp.concatenate([pr * win[0] - pi * win[1], pr * win[1] + pi * win[0]], axis=1)
                )
            wins.append(win)
            probes.append(probe)
            places.append((p, row, block, shift, slot))
        half = right_product(jnp.concatenate(waves, axis=0), factors, 0)
        columns = []
        for k in range(SLOTS_AT_ONCE * modes):
            rows = half[k * points : (k + 1) * points]
            columns.append(jnp.concatenate([rows[:, :points], rows[:, points:]], axis=0))
        spec = left_product(factors, 2, jnp.concatenate(columns, axis=1))
        columns = []
        for u in range(SLOTS_AT_ONCE):
            own = [spec[:, (u * modes + m) * points : (u * modes + m + 1) * points] for m in range(modes)]
            total = functools.reduce(jnp.add, [s * s for s in own])
            intensity = total[:points] + total[points:]
            factor = amplitudes[places[u][0]] * lax.rsqrt(jnp.maximum(intensity, floor_level * floor_level)) - 1.0
            factor = factor * flags[u]
            factor = jnp.concatenate([factor, factor], axis=0)
            columns += [s * factor for s in own]
        half = left_product(factors, 0, jnp.concatenate(columns, axis=1))
        rows = []
        for k in range(SLOTS_AT_ONCE * modes):
            column = half[:, k * points : (k + 1) * points]
            rows.append(jnp.concatenate([column[:points], column[points:]], axis=1))
        change = right_product(jnp.concatenate(rows, axis=0), factors, 2)
        for u in range(SLOTS_AT_ONCE):
            p, row, block, shift, slot = places[u]
            wr, wi = wins[u]
            term_r = term_i = None
            for m in range(modes):
                k = u * modes + m
                pr, pi = probes[u][m]
                dr = change[k * points : (k + 1) * points, :points]
                di = change[k * points : (k + 1) * points, points:]
                tr, ti = pr * dr + pi * di, pr * di - pi * dr
                term_r = tr if m == 0 else term_r + tr
                term_i = ti if m == 0 else term_i + ti
                part[slot, 2 * m] += wr * dr + wi * di
                part[slot, 2 * m + 1] += wr * di - wi * dr
            part[slot, 2 * modes] += (wr * wr + wi * wi) * flags[u]
            first = lane >= shift
            for ch, term in enumerate((term_r, term_i)):
                term = pltpu.roll(term, shift, 1)
                acc[ch, block, pl.ds(row, points), :] += jnp.where(first, term, 0.0)
                acc[ch, block + 1, pl.ds(row, points), :] += jnp.where(first, 0.0, term)
        return carry

    lax.fori_loop(0, (count + SLOTS_AT_ONCE - 1) // SLOTS_AT_ONCE, step, 0)

    copies = []
    at = 0
    for k, size in enumerate(group_sizes):
        copies.append(pltpu.make_async_copy(part.at[pl.ds(at, size)], groups[k], out_sems.at[k]))
        at += size
    k = len(group_sizes)
    copies.append(
        pltpu.make_async_copy(acc.at[:, pl.ds(0, blocks), pl.ds(tile_rows, points), :], num_low, out_sems.at[k])
    )
    copies.append(
        pltpu.make_async_copy(acc.at[:, pl.ds(0, blocks), pl.ds(0, tile_rows), :], num_top, out_sems.at[k + 1])
    )
    for copy in copies:
        copy.start()
    for copy in copies:
        copy.wait()


def update(meta, slot_of, live, amplitudes, obj, rim, factors, pieces, group_sizes):
    points = amplitudes.shape[-1]
    tile_rows = obj.shape[1]
    blocks = obj.shape[2] // LANES
    channels = pieces[0].shape[1]
    scans = slot_of.shape[0]
    piece_sizes = tuple(piece.shape[0] for piece in pieces)
    slots = sum(piece_sizes)
    f32 = jnp.float32
    smem = pl.BlockSpec(memory_space=pltpu.SMEM)
    vmem = pl.BlockSpec(memory_space=pltpu.VMEM)
    anywhere = pl.BlockSpec(memory_space=pl.ANY)
    return pl.pallas_call(
        functools.partial(update_kernel, (piece_sizes, group_sizes, slots)),
        out_shape=[
            jax.ShapeDtypeStruct((2, blocks, tile_rows, LANES), f32),
            jax.ShapeDtypeStruct((2, blocks, points, LANES), f32),
            jax.ShapeDtypeStruct((scans, points, points), f32),
        ]
        + [jax.ShapeDtypeStruct((size, channels + 1, points, points), f32) for size in group_sizes],
        in_specs=[smem] * 3 + [vmem, anywhere, anywhere, vmem] + [anywhere] * len(pieces),
        out_specs=[anywhere, anywhere, vmem] + [anywhere] * len(group_sizes),
        scratch_shapes=[
            pltpu.VMEM((slots, channels, points, points), f32),
            pltpu.VMEM((2, blocks + 1, tile_rows + points, LANES), f32),
            pltpu.VMEM((2, blocks + 1, tile_rows + points, LANES), f32),
            pltpu.VMEM((slots, channels + 1, points, points), f32),
            pltpu.SemaphoreType.DMA((len(pieces) + 2 * blocks,)),
            pltpu.SemaphoreType.DMA((len(group_sizes) + 2,)),
        ],
        compiler_params=pltpu.CompilerParams(vmem_limit_bytes=VMEM_BYTES),
        cost_estimate=pl.CostEstimate(flops=6 * 10**9, bytes_accessed=16 * 2**20, transcendentals=2**18),
        name="update",
    )(meta, slot_of, live, amplitudes, obj, rim, factors, *pieces)


def density_kernel(tile_rows, meta, above, squares, density, ext):
    points = LANES
    blocks = density.shape[0]
    ext[...] = jnp.zeros_like(ext)
    lane = lax.broadcasted_iota(jnp.int32, (points, LANES), 1)

    def place(values, row, col):
        block, shift = col // LANES, col % LANES
        first = lane >= shift
        values = pltpu.roll(values, shift, 1)
        ext[block, pl.ds(row, points), :] += jnp.where(first, values, 0.0)
        ext[block + 1, pl.ds(row, points), :] += jnp.where(first, 0.0, values)

    def own(p, carry):
        @pl.when(meta[4 * p + 3] > 0)
        def _():
            place(squares[meta[4 * p + 2]], meta[4 * p] + points, meta[4 * p + 1])

        return carry

    def upper(p, carry):
        row = above[4 * p] - tile_rows + points

        @pl.when((above[4 * p + 3] > 0) & (row > 0))
        def _():
            place(squares[above[4 * p + 2]], row, above[4 * p + 1])

        return carry

    lax.fori_loop(0, meta.shape[0] // 4, own, 0)
    lax.fori_loop(0, above.shape[0] // 4, upper, 0)
    density[...] = ext[:blocks, points : points + tile_rows, :]


def density_of(meta, above, squares, tile_rows, blocks):
    points = squares.shape[-1]
    smem = pl.BlockSpec(memory_space=pltpu.SMEM)
    vmem = pl.BlockSpec(memory_space=pltpu.VMEM)
    return pl.pallas_call(
        functools.partial(density_kernel, tile_rows),
        out_shape=jax.ShapeDtypeStruct((blocks, tile_rows, LANES), jnp.float32),
        in_specs=[smem, smem, vmem],
        out_specs=vmem,
        scratch_shapes=[pltpu.VMEM((blocks + 1, points + tile_rows + points, LANES), jnp.float32)],
        compiler_params=pltpu.CompilerParams(vmem_limit_bytes=VMEM_BYTES),
        cost_estimate=pl.CostEstimate(flops=2**23, bytes_accessed=8 * 2**20, transcendentals=0),
        name="density",
    )(meta, above, squares)


def finish_kernel(obj, num_top, received, density, out):
    points = received.shape[2]
    for b in range(density.shape[0]):
        columns = slice(b * LANES, (b + 1) * LANES)
        scale = 1.0 / (density[b] + damping)
        for ch in range(2):
            head = num_top[ch, b, :points] + received[ch, b]
            out[ch, :points, columns] = obj[ch, :points, columns] + head * scale[:points]
            out[ch, points:, columns] = obj[ch, points:, columns] + num_top[ch, b, points:] * scale[points:]


def finish(obj, num_top, received, density):
    vmem = pl.BlockSpec(memory_space=pltpu.VMEM)
    return pl.pallas_call(
        finish_kernel,
        out_shape=jax.ShapeDtypeStruct(obj.shape, obj.dtype),
        in_specs=[vmem] * 4,
        out_specs=vmem,
        compiler_params=pltpu.CompilerParams(vmem_limit_bytes=VMEM_BYTES),
        cost_estimate=pl.CostEstimate(flops=2**21, bytes_accessed=8 * 2**20, transcendentals=0),
        name="finish",
    )(obj, num_top, received, density)


def staged_kernel(*refs):
    half = (len(refs) - 1) // 2
    copies = [pltpu.make_async_copy(refs[k], refs[half + k], refs[-1].at[k]) for k in range(half)]
    for copy in copies:
        copy.start()
    for copy in copies:
        copy.wait()


def staged(*arrays):
    return pl.pallas_call(
        staged_kernel,
        out_shape=[jax.ShapeDtypeStruct(array.shape, array.dtype) for array in arrays],
        in_specs=[pl.BlockSpec(memory_space=pl.ANY)] * len(arrays),
        out_specs=[pl.BlockSpec(memory_space=pltpu.VMEM)] * len(arrays),
        scratch_shapes=[pltpu.SemaphoreType.DMA((len(arrays),))],
        compiler_params=pltpu.CompilerParams(vmem_limit_bytes=VMEM_BYTES),
        name="staged",
    )(*arrays)


def local(object_strip, probe_store, amplitudes, scan_of, offsets, counts, owner):
    device = lax.axis_index("row")
    size = lax.axis_size("row")
    tile_rows = object_strip.shape[1]
    blocks = object_strip.shape[2] // LANES
    points = probe_store.shape[-1]
    modes = probe_store.shape[1]
    slot_count = amplitudes.shape[0]
    scan_count = owner.shape[0]
    channels = 2 * modes
    swaps = size == 16
    own_probe = probe_store.reshape(1, channels, points, points)

    is_live = (jnp.arange(slot_count, dtype=jnp.int32) < counts[0]).astype(jnp.int32)
    meta = jnp.stack([offsets[:, 0] - device * tile_rows, offsets[:, 1], scan_of, is_live], axis=1).reshape(-1)

    if swaps:
        held = {0: own_probe}
        for key in (8, 4, 2):
            held[key] = swapped(own_probe, key)
        held[8], held[4], held[2] = lax.optimization_barrier((held[8], held[4], held[2]))
        held[6] = swapped(held[4], 2)
        held[12] = swapped(held[8], 4)
        held[10] = swapped(held[8], 2)
        held[14] = swapped(held[12], 2)
        for key in list(held):
            held[key | 1] = swapped(held[key], 1)
        order = [key | core for core in (0, 1) for key in FAR + NEAR]
        amplitudes, factors, held[0] = staged(amplitudes, after(transform_tables(points), held[12]), own_probe)
        pieces = [held[key] for key in order]
        key = jnp.bitwise_xor(owner, device)
        side = key // 2 % 4
        slot_of = key % 2 * 8 + (1 - key // 8) * 4 + jnp.bitwise_xor(side, side // 2)
        group_sizes = (4,) * 4
    else:
        owned = (owner == device)[:, None, None, None]
        pieces = [lax.psum(jnp.where(owned, own_probe, 0.0), "row")]
        slot_of = jnp.arange(scan_count, dtype=jnp.int32)
        group_sizes = (scan_count,)
        factors = transform_tables(points)

    rim = moved(after(object_strip[:, :points, :], slot_of), -1)
    above = moved(after(meta, held[7]) if swaps else meta, 1)
    rim = after(rim, above)
    num_top, num_low, squares, *groups = update(
        meta, slot_of, counts, amplitudes, object_strip, rim, factors, pieces, group_sizes
    )

    density = density_of(meta, above, squares, tile_rows, blocks)
    if swaps:
        mine_far, mine_near, theirs_far, theirs_near = groups
        total, received, density = reduced((mine_far, swapped(theirs_far, 1)), theirs_near, mine_near, num_low, density)
    else:
        received = moved(num_low, 1)
        summed = lax.psum(groups[0], "row")
        total = jnp.sum(jnp.where(owned, summed, 0.0), axis=0)
    new_object = finish(object_strip, num_top, received, density)
    new_probes = own_probe[0] + total[:channels] / (total[channels] + damping)
    return (new_object, new_probes.reshape(probe_store.shape))


def solution(mesh):
    return jax.shard_map(
        local,
        mesh=mesh,
        in_specs=(
            P(None, ("grp", "row"), None),
            P(("grp", "row"), None, None, None, None),
            P(("grp", "row"), None, None),
            P(("grp", "row")),
            P(("grp", "row"), None),
            P(("grp", "row")),
            P("grp"),
        ),
        out_specs=(P(None, ("grp", "row"), None), P(("grp", "row"), None, None, None, None)),
        check_vma=False,
    )
```

```python
import functools
import math

import jax
import jax.numpy as jnp
import numpy as np
from jax import lax
from jax.experimental import pallas as pl
from jax.experimental.pallas import tpu as pltpu
from jax.sharding import PartitionSpec as P

damping = 1.0
floor_level = 0.3
LANES = 128
SLOTS_AT_ONCE = 8
VMEM_BYTES = 26 * 1024 * 1024


def moved(block, distance):
    size = lax.axis_size("row")
    return lax.ppermute(block, "row", [(i, i + distance) for i in range(size) if 0 <= i + distance < size])


def swapped(block, mask):
    return lax.ppermute(block, "row", [(i, i ^ mask) for i in range(lax.axis_size("row"))])


FAR, NEAR = (8, 10, 14, 12), (0, 2, 6, 4)


def reduced(far, theirs_near, mine_near, low, density):
    half = far[0].shape[2] // 2
    routes = ((slice(0, half), 2, 4, (1, 2), 3), (slice(half, 2 * half), 4, 2, (3, 2), 1))

    def pick(pair, at, rows):
        return pair[0][at, :, rows] + pair[1][at, :, rows]

    def first_step(pair):
        return [swapped(jnp.stack([pick(pair, at, rows) for at in sent]), mask) for rows, mask, _, sent, _ in routes]

    got = first_step(far)
    near = (mine_near, swapped(theirs_near, 1))
    got_near = first_step(near)
    low = after(low, *got)
    received = moved(low, 1)
    outer, across = [], []
    for (rows, _, second, _, kept), arrived in zip(routes, got):
        outer.append(pick(far, 0, rows) + arrived[0])
        across.append(pick(far, kept, rows) + arrived[1])
    density, across[0] = lax.optimization_barrier((density, across[0]))
    across = [swapped(block, route[2]) for block, route in zip(across, routes)]
    beside = []
    for (rows, _, second, _, kept), arrived in zip(routes, got_near):
        beside.append(swapped(pick(near, kept, rows) + arrived[1], second))
    totals = []
    for k, (rows, _, _, _, _) in enumerate(routes):
        ahead = swapped(outer[k] + across[k], 8)
        totals.append(pick(near, 0, rows) + got_near[k][0] + beside[k] + ahead)
    return jnp.concatenate(totals, axis=1), received, density


def after(value, *others):
    return lax.optimization_barrier((value,) + others)[0]


def split(value):
    high = value.astype(jnp.bfloat16)
    low = (value - high.astype(jnp.float32)).astype(jnp.bfloat16)
    return high, low


def transform_tables(points):
    index = np.arange(points)
    angle = (index[:, None] * index[None, :] % points) * (2.0 * math.pi / points)
    cos, sin = np.cos(angle) / math.sqrt(points), np.sin(angle) / math.sqrt(points)
    minus = np.block([[cos, -sin], [sin, cos]])
    plus = np.block([[cos, sin], [-sin, cos]])

    parts = []
    for matrix in (minus.astype(np.float32), plus.astype(np.float32)):
        high = matrix.astype(jnp.bfloat16)
        parts += [high, (matrix - high.astype(np.float32)).astype(jnp.bfloat16)]
    return jnp.asarray(np.stack(parts))


def right_product(rows, factor, at):
    high, low = split(rows)
    table = jnp.concatenate([factor[at], factor[at], factor[at + 1]], axis=0)
    return jnp.dot(jnp.concatenate([high, low, high], axis=1), table, preferred_element_type=jnp.float32)


def left_product(factor, at, columns):
    high, low = split(columns)
    table = jnp.concatenate([factor[at], factor[at], factor[at + 1]], axis=1)
    return jnp.dot(table, jnp.concatenate([high, low, high], axis=0), preferred_element_type=jnp.float32)


def update_kernel(dims, meta, slot_of, live, amplitudes, obj, rim, factors, *rest):
    piece_sizes, group_sizes, slots = dims
    pieces = rest[: len(piece_sizes)]
    rest = rest[len(piece_sizes) :]
    num_top, num_low, squares = rest[:3]
    groups = rest[3 : 3 + len(group_sizes)]
    table, ext, acc, part, in_sems, out_sems = rest[3 + len(group_sizes) :]
    points = LANES
    tile_rows = obj.shape[1]
    blocks = obj.shape[2] // LANES
    modes = table.shape[1] // 2

    moves = []
    for b in range(blocks):
        columns = pl.ds(b * LANES, LANES)
        moves.append((obj.at[:, :, columns], ext.at[:, b, pl.ds(0, tile_rows), :]))
        moves.append((rim.at[:, :, columns], ext.at[:, b, pl.ds(tile_rows, points), :]))
    at = 0
    for k, size in enumerate(piece_sizes):
        moves.append((pieces[k], table.at[pl.ds(at, size)]))
        at += size
    copies = [pltpu.make_async_copy(*ends, in_sems.at[k]) for k, ends in enumerate(moves)]
    for copy in copies:
        copy.start()
    acc[...] = jnp.zeros_like(acc)
    part[...] = jnp.zeros_like(part)
    for copy in copies:
        copy.wait()
    for s in range(squares.shape[0]):
        probe = table[slot_of[s]]
        squares[s] = jnp.sum(probe * probe, axis=0)

    lane = lax.broadcasted_iota(jnp.int32, (points, LANES), 1)
    count = live[0]

    def step(i, carry):
        wins, probes, places, waves, flags = [], [], [], [], []
        for u in range(SLOTS_AT_ONCE):
            at = i * SLOTS_AT_ONCE + u
            flags.append((at < count).astype(jnp.float32))
            p = jnp.minimum(at, count - 1)
            row, col, scan = meta[4 * p], meta[4 * p + 1], meta[4 * p + 2]
            slot = slot_of[scan]
            block, shift = col // LANES, col % LANES
            back = lax.rem(LANES - shift, LANES)
            keep = lane >= shift
            win = []
            for ch in range(2):
                first = ext[ch, block, pl.ds(row, points), :]
                second = ext[ch, block + 1, pl.ds(row, points), :]
                win.append(pltpu.roll(jnp.where(keep, first, second), back, 1))
            probe = [(table[slot, 2 * m], table[slot, 2 * m + 1]) for m in range(modes)]
            for pr, pi in probe:
                waves.append(
                    jnp.concatenate([pr * win[0] - pi * win[1], pr * win[1] + pi * win[0]], axis=1)
                )
            wins.append(win)
            probes.append(probe)
            places.append((p, row, block, shift, slot))
        half = right_product(jnp.concatenate(waves, axis=0), factors, 0)
        columns = []
        for k in range(SLOTS_AT_ONCE * modes):
            rows = half[k * points : (k + 1) * points]
            columns.append(jnp.concatenate([rows[:, :points], rows[:, points:]], axis=0))
        spec = left_product(factors, 2, jnp.concatenate(columns, axis=1))
        columns = []
        for u in range(SLOTS_AT_ONCE):
            own = [spec[:, (u * modes + m) * points : (u * modes + m + 1) * points] for m in range(modes)]
            total = functools.reduce(jnp.add, [s * s for s in own])
            intensity = total[:points] + total[points:]
            factor = amplitudes[places[u][0]] * lax.rsqrt(jnp.maximum(intensity, floor_level * floor_level)) - 1.0
            factor = factor * flags[u]
            factor = jnp.concatenate([factor, factor], axis=0)
            columns += [s * factor for s in own]
        half = left_product(factors, 0, jnp.concatenate(columns, axis=1))
        rows = []
        for k in range(SLOTS_AT_ONCE * modes):
            column = half[:, k * points : (k + 1) * points]
            rows.append(jnp.concatenate([column[:points], column[points:]], axis=1))
        change = right_product(jnp.concatenate(rows, axis=0), factors, 2)
        for u in range(SLOTS_AT_ONCE):
            p, row, block, shift, slot = places[u]
            wr, wi = wins[u]
            term_r = term_i = None
            for m in range(modes):
                k = u * modes + m
                pr, pi = probes[u][m]
                dr = change[k * points : (k + 1) * points, :points]
                di = change[k * points : (k + 1) * points, points:]
                tr, ti = pr * dr + pi * di, pr * di - pi * dr
                term_r = tr if m == 0 else term_r + tr
                term_i = ti if m == 0 else term_i + ti
                part[slot, 2 * m] += wr * dr + wi * di
                part[slot, 2 * m + 1] += wr * di - wi * dr
            part[slot, 2 * modes] += (wr * wr + wi * wi) * flags[u]
            first = lane >= shift
            for ch, term in enumerate((term_r, term_i)):
                term = pltpu.roll(term, shift, 1)
                acc[ch, block, pl.ds(row, points), :] += jnp.where(first, term, 0.0)
                acc[ch, block + 1, pl.ds(row, points), :] += jnp.where(first, 0.0, term)
        return carry

    lax.fori_loop(0, (count + SLOTS_AT_ONCE - 1) // SLOTS_AT_ONCE, step, 0)

    copies = []
    at = 0
    for k, size in enumerate(group_sizes):
        copies.append(pltpu.make_async_copy(part.at[pl.ds(at, size)], groups[k], out_sems.at[k]))
        at += size
    k = len(group_sizes)
    copies.append(
        pltpu.make_async_copy(acc.at[:, pl.ds(0, blocks), pl.ds(tile_rows, points), :], num_low, out_sems.at[k])
    )
    copies.append(
        pltpu.make_async_copy(acc.at[:, pl.ds(0, blocks), pl.ds(0, tile_rows), :], num_top, out_sems.at[k + 1])
    )
    for copy in copies:
        copy.start()
    for copy in copies:
        copy.wait()


def update(meta, slot_of, live, amplitudes, obj, rim, factors, pieces, group_sizes):
    points = amplitudes.shape[-1]
    tile_rows = obj.shape[1]
    blocks = obj.shape[2] // LANES
    channels = pieces[0].shape[1]
    scans = slot_of.shape[0]
    piece_sizes = tuple(piece.shape[0] for piece in pieces)
    slots = sum(piece_sizes)
    f32 = jnp.float32
    smem = pl.BlockSpec(memory_space=pltpu.SMEM)
    vmem = pl.BlockSpec(memory_space=pltpu.VMEM)
    anywhere = pl.BlockSpec(memory_space=pl.ANY)
    return pl.pallas_call(
        functools.partial(update_kernel, (piece_sizes, group_sizes, slots)),
        out_shape=[
            jax.ShapeDtypeStruct((2, blocks, tile_rows, LANES), f32),
            jax.ShapeDtypeStruct((2, blocks, points, LANES), f32),
            jax.ShapeDtypeStruct((scans, points, points), f32),
        ]
        + [jax.ShapeDtypeStruct((size, channels + 1, points, points), f32) for size in group_sizes],
        in_specs=[smem] * 3 + [vmem, anywhere, anywhere, vmem] + [anywhere] * len(pieces),
        out_specs=[anywhere, anywhere, vmem] + [anywhere] * len(group_sizes),
        scratch_shapes=[
            pltpu.VMEM((slots, channels, points, points), f32),
            pltpu.VMEM((2, blocks + 1, tile_rows + points, LANES), f32),
            pltpu.VMEM((2, blocks + 1, tile_rows + points, LANES), f32),
            pltpu.VMEM((slots, channels + 1, points, points), f32),
            pltpu.SemaphoreType.DMA((len(pieces) + 2 * blocks,)),
            pltpu.SemaphoreType.DMA((len(group_sizes) + 2,)),
        ],
        compiler_params=pltpu.CompilerParams(vmem_limit_bytes=VMEM_BYTES),
        cost_estimate=pl.CostEstimate(flops=6 * 10**9, bytes_accessed=16 * 2**20, transcendentals=2**18),
        name="update",
    )(meta, slot_of, live, amplitudes, obj, rim, factors, *pieces)


def density_kernel(tile_rows, meta, above, squares, density, ext):
    points = LANES
    blocks = density.shape[0]
    ext[...] = jnp.zeros_like(ext)
    lane = lax.broadcasted_iota(jnp.int32, (points, LANES), 1)

    def place(values, row, col):
        block, shift = col // LANES, col % LANES
        first = lane >= shift
        values = pltpu.roll(values, shift, 1)
        ext[block, pl.ds(row, points), :] += jnp.where(first, values, 0.0)
        ext[block + 1, pl.ds(row, points), :] += jnp.where(first, 0.0, values)

    def own(p, carry):
        @pl.when(meta[4 * p + 3] > 0)
        def _():
            place(squares[meta[4 * p + 2]], meta[4 * p] + points, meta[4 * p + 1])

        return carry

    def upper(p, carry):
        row = above[4 * p] - tile_rows + points

        @pl.when((above[4 * p + 3] > 0) & (row > 0))
        def _():
            place(squares[above[4 * p + 2]], row, above[4 * p + 1])

        return carry

    lax.fori_loop(0, meta.shape[0] // 4, own, 0)
    lax.fori_loop(0, above.shape[0] // 4, upper, 0)
    density[...] = ext[:blocks, points : points + tile_rows, :]


def density_of(meta, above, squares, tile_rows, blocks):
    points = squares.shape[-1]
    smem = pl.BlockSpec(memory_space=pltpu.SMEM)
    vmem = pl.BlockSpec(memory_space=pltpu.VMEM)
    return pl.pallas_call(
        functools.partial(density_kernel, tile_rows),
        out_shape=jax.ShapeDtypeStruct((blocks, tile_rows, LANES), jnp.float32),
        in_specs=[smem, smem, vmem],
        out_specs=vmem,
        scratch_shapes=[pltpu.VMEM((blocks + 1, points + tile_rows + points, LANES), jnp.float32)],
        compiler_params=pltpu.CompilerParams(vmem_limit_bytes=VMEM_BYTES),
        cost_estimate=pl.CostEstimate(flops=2**23, bytes_accessed=8 * 2**20, transcendentals=0),
        name="density",
    )(meta, above, squares)


def finish_kernel(obj, num_top, received, density, out):
    points = received.shape[2]
    for b in range(density.shape[0]):
        columns = slice(b * LANES, (b + 1) * LANES)
        scale = 1.0 / (density[b] + damping)
        for ch in range(2):
            head = num_top[ch, b, :points] + received[ch, b]
            out[ch, :points, columns] = obj[ch, :points, columns] + head * scale[:points]
            out[ch, points:, columns] = obj[ch, points:, columns] + num_top[ch, b, points:] * scale[points:]


def finish(obj, num_top, received, density):
    vmem = pl.BlockSpec(memory_space=pltpu.VMEM)
    return pl.pallas_call(
        finish_kernel,
        out_shape=jax.ShapeDtypeStruct(obj.shape, obj.dtype),
        in_specs=[vmem] * 4,
        out_specs=vmem,
        compiler_params=pltpu.CompilerParams(vmem_limit_bytes=VMEM_BYTES),
        cost_estimate=pl.CostEstimate(flops=2**21, bytes_accessed=8 * 2**20, transcendentals=0),
        name="finish",
    )(obj, num_top, received, density)


def staged_kernel(*refs):
    half = (len(refs) - 1) // 2
    copies = [pltpu.make_async_copy(refs[k], refs[half + k], refs[-1].at[k]) for k in range(half)]
    for copy in copies:
        copy.start()
    for copy in copies:
        copy.wait()


def staged(*arrays):
    return pl.pallas_call(
        staged_kernel,
        out_shape=[jax.ShapeDtypeStruct(array.shape, array.dtype) for array in arrays],
        in_specs=[pl.BlockSpec(memory_space=pl.ANY)] * len(arrays),
        out_specs=[pl.BlockSpec(memory_space=pltpu.VMEM)] * len(arrays),
        scratch_shapes=[pltpu.SemaphoreType.DMA((len(arrays),))],
        compiler_params=pltpu.CompilerParams(vmem_limit_bytes=VMEM_BYTES),
        name="staged",
    )(*arrays)


def local(object_strip, probe_store, amplitudes, scan_of, offsets, counts, owner):
    device = lax.axis_index("row")
    size = lax.axis_size("row")
    tile_rows = object_strip.shape[1]
    blocks = object_strip.shape[2] // LANES
    points = probe_store.shape[-1]
    modes = probe_store.shape[1]
    slot_count = amplitudes.shape[0]
    scan_count = owner.shape[0]
    channels = 2 * modes
    swaps = size == 16
    own_probe = probe_store.reshape(1, channels, points, points)

    is_live = (jnp.arange(slot_count, dtype=jnp.int32) < counts[0]).astype(jnp.int32)
    meta = jnp.stack([offsets[:, 0] - device * tile_rows, offsets[:, 1], scan_of, is_live], axis=1).reshape(-1)

    if swaps:
        held = {0: own_probe}
        for key in (8, 4, 2):
            held[key] = swapped(own_probe, key)
        held[8], held[4], held[2] = lax.optimization_barrier((held[8], held[4], held[2]))
        held[6] = swapped(held[2], 4)
        held[12] = swapped(held[8], 4)
        held[10] = swapped(held[8], 2)
        held[14] = swapped(held[10], 4)
        for key in list(held):
            held[key | 1] = swapped(held[key], 1)
        order = [key | core for core in (0, 1) for key in FAR + NEAR]
        amplitudes, factors, held[0] = staged(amplitudes, after(transform_tables(points), held[12]), own_probe)
        pieces = [held[key] for key in order]
        key = jnp.bitwise_xor(owner, device)
        side = key // 2 % 4
        slot_of = key % 2 * 8 + (1 - key // 8) * 4 + jnp.bitwise_xor(side, side // 2)
        group_sizes = (4,) * 4
    else:
        owned = (owner == device)[:, None, None, None]
        pieces = [lax.psum(jnp.where(owned, own_probe, 0.0), "row")]
        slot_of = jnp.arange(scan_count, dtype=jnp.int32)
        group_sizes = (scan_count,)
        factors = transform_tables(points)

    rim = moved(after(object_strip[:, :points, :], slot_of), -1)
    above = moved(after(meta, held[7]) if swaps else meta, 1)
    rim = after(rim, above)
    num_top, num_low, squares, *groups = update(
        meta, slot_of, counts, amplitudes, object_strip, rim, factors, pieces, group_sizes
    )

    density = density_of(meta, above, squares, tile_rows, blocks)
    if swaps:
        mine_far, mine_near, theirs_far, theirs_near = groups
        total, received, density = reduced((mine_far, swapped(theirs_far, 1)), theirs_near, mine_near, num_low, density)
    else:
        received = moved(num_low, 1)
        summed = lax.psum(groups[0], "row")
        total = jnp.sum(jnp.where(owned, summed, 0.0), axis=0)
    new_object = finish(object_strip, num_top, received, density)
    new_probes = own_probe[0] + total[:channels] / (total[channels] + damping)
    return (new_object, new_probes.reshape(probe_store.shape))


def solution(mesh):
    return jax.shard_map(
        local,
        mesh=mesh,
        in_specs=(
            P(None, ("grp", "row"), None),
            P(("grp", "row"), None, None, None, None),
            P(("grp", "row"), None, None),
            P(("grp", "row")),
            P(("grp", "row"), None),
            P(("grp", "row")),
            P("grp"),
        ),
        out_specs=(P(None, ("grp", "row"), None), P(("grp", "row"), None, None, None, None)),
        check_vma=False,
    )
```

```python
import functools
import math

import jax
import jax.numpy as jnp
import numpy as np
from jax import lax
from jax.experimental import pallas as pl
from jax.experimental.pallas import tpu as pltpu
from jax.sharding import PartitionSpec as P

damping = 1.0
floor_level = 0.3
LANES = 128
SLOTS_AT_ONCE = 8
VMEM_BYTES = 26 * 1024 * 1024


def moved(block, distance):
    size = lax.axis_size("row")
    return lax.ppermute(block, "row", [(i, i + distance) for i in range(size) if 0 <= i + distance < size])


def swapped(block, mask):
    return lax.ppermute(block, "row", [(i, i ^ mask) for i in range(lax.axis_size("row"))])


FAR, NEAR = (8, 10, 14, 12), (0, 2, 6, 4)


def reduced(far, theirs_near, mine_near, low, density):
    half = far[0].shape[2] // 2
    routes = ((slice(0, half), 2, 4, (1, 2), 3), (slice(half, 2 * half), 4, 2, (3, 2), 1))

    def pick(pair, at, rows):
        return pair[0][at, :, rows] + pair[1][at, :, rows]

    def first_step(pair):
        return [swapped(jnp.stack([pick(pair, at, rows) for at in sent]), mask) for rows, mask, _, sent, _ in routes]

    got = first_step(far)
    near = (mine_near, swapped(theirs_near, 1))
    got_near = first_step(near)
    low = after(low, *got)
    received = moved(low, 1)
    outer, across = [], []
    for (rows, _, second, _, kept), arrived in zip(routes, got):
        outer.append(pick(far, 0, rows) + arrived[0])
        across.append(pick(far, kept, rows) + arrived[1])
    density, across[0] = lax.optimization_barrier((density, across[0]))
    across = [swapped(block, route[2]) for block, route in zip(across, routes)]
    beside = []
    for (rows, _, second, _, kept), arrived in zip(routes, got_near):
        beside.append(swapped(pick(near, kept, rows) + arrived[1], second))
    totals = []
    for k, (rows, _, _, _, _) in enumerate(routes):
        ahead = swapped(outer[k] + across[k], 8)
        totals.append(pick(near, 0, rows) + got_near[k][0] + beside[k] + ahead)
    return jnp.concatenate(totals, axis=1), received, density


def after(value, *others):
    return lax.optimization_barrier((value,) + others)[0]


def split(value):
    high = value.astype(jnp.bfloat16)
    low = (value - high.astype(jnp.float32)).astype(jnp.bfloat16)
    return high, low


def transform_tables(points):
    index = np.arange(points)
    angle = (index[:, None] * index[None, :] % points) * (2.0 * math.pi / points)
    cos, sin = np.cos(angle) / math.sqrt(points), np.sin(angle) / math.sqrt(points)
    minus = np.block([[cos, -sin], [sin, cos]])
    plus = np.block([[cos, sin], [-sin, cos]])

    parts = []
    for matrix in (minus.astype(np.float32), plus.astype(np.float32)):
        high = matrix.astype(jnp.bfloat16)
        parts += [high, (matrix - high.astype(np.float32)).astype(jnp.bfloat16)]
    return jnp.asarray(np.stack(parts))


def right_product(rows, factor, at):
    high, low = split(rows)
    table = jnp.concatenate([factor[at], factor[at], factor[at + 1]], axis=0)
    return jnp.dot(jnp.concatenate([high, low, high], axis=1), table, preferred_element_type=jnp.float32)


def left_product(factor, at, columns):
    high, low = split(columns)
    table = jnp.concatenate([factor[at], factor[at], factor[at + 1]], axis=1)
    return jnp.dot(table, jnp.concatenate([high, low, high], axis=0), preferred_element_type=jnp.float32)


def update_kernel(dims, meta, slot_of, live, amplitudes, obj, rim, factors, *rest):
    piece_sizes, group_sizes, slots = dims
    pieces = rest[: len(piece_sizes)]
    rest = rest[len(piece_sizes) :]
    num_top, num_low, squares = rest[:3]
    groups = rest[3 : 3 + len(group_sizes)]
    table, ext, acc, part, in_sems, out_sems = rest[3 + len(group_sizes) :]
    points = LANES
    tile_rows = obj.shape[1]
    blocks = obj.shape[2] // LANES
    modes = table.shape[1] // 2

    moves = []
    for b in range(blocks):
        columns = pl.ds(b * LANES, LANES)
        moves.append((obj.at[:, :, columns], ext.at[:, b, pl.ds(0, tile_rows), :]))
        moves.append((rim.at[:, :, columns], ext.at[:, b, pl.ds(tile_rows, points), :]))
    at = 0
    for k, size in enumerate(piece_sizes):
        moves.append((pieces[k], table.at[pl.ds(at, size)]))
        at += size
    copies = [pltpu.make_async_copy(*ends, in_sems.at[k]) for k, ends in enumerate(moves)]
    for copy in copies:
        copy.start()
    acc[...] = jnp.zeros_like(acc)
    part[...] = jnp.zeros_like(part)
    for copy in copies:
        copy.wait()
    for s in range(squares.shape[0]):
        probe = table[slot_of[s]]
        squares[s] = jnp.sum(probe * probe, axis=0)

    lane = lax.broadcasted_iota(jnp.int32, (points, LANES), 1)
    count = live[0]

    def step(i, carry):
        wins, probes, places, waves, flags = [], [], [], [], []
        for u in range(SLOTS_AT_ONCE):
            at = i * SLOTS_AT_ONCE + u
            flags.append((at < count).astype(jnp.float32))
            p = jnp.minimum(at, count - 1)
            row, col, scan = meta[4 * p], meta[4 * p + 1], meta[4 * p + 2]
            slot = slot_of[scan]
            block, shift = col // LANES, col % LANES
            back = lax.rem(LANES - shift, LANES)
            keep = lane >= shift
            win = []
            for ch in range(2):
                first = ext[ch, block, pl.ds(row, points), :]
                second = ext[ch, block + 1, pl.ds(row, points), :]
                win.append(pltpu.roll(jnp.where(keep, first, second), back, 1))
            probe = [(table[slot, 2 * m], table[slot, 2 * m + 1]) for m in range(modes)]
            for pr, pi in probe:
                waves.append(
                    jnp.concatenate([pr * win[0] - pi * win[1], pr * win[1] + pi * win[0]], axis=1)
                )
            wins.append(win)
            probes.append(probe)
            places.append((p, row, block, shift, slot))
        half = right_product(jnp.concatenate(waves, axis=0), factors, 0)
        columns = []
        for k in range(SLOTS_AT_ONCE * modes):
            rows = half[k * points : (k + 1) * points]
            columns.append(jnp.concatenate([rows[:, :points], rows[:, points:]], axis=0))
        spec = left_product(factors, 2, jnp.concatenate(columns, axis=1))
        columns = []
        for u in range(SLOTS_AT_ONCE):
            own = [spec[:, (u * modes + m) * points : (u * modes + m + 1) * points] for m in range(modes)]
            total = functools.reduce(jnp.add, [s * s for s in own])
            intensity = total[:points] + total[points:]
            factor = amplitudes[places[u][0]] * lax.rsqrt(jnp.maximum(intensity, floor_level * floor_level)) - 1.0
            factor = factor * flags[u]
            factor = jnp.concatenate([factor, factor], axis=0)
            columns += [s * factor for s in own]
        half = left_product(factors, 0, jnp.concatenate(columns, axis=1))
        rows = []
        for k in range(SLOTS_AT_ONCE * modes):
            column = half[:, k * points : (k + 1) * points]
            rows.append(jnp.concatenate([column[:points], column[points:]], axis=1))
        change = right_product(jnp.concatenate(rows, axis=0), factors, 2)
        for u in range(SLOTS_AT_ONCE):
            p, row, block, shift, slot = places[u]
            wr, wi = wins[u]
            term_r = term_i = None
            for m in range(modes):
                k = u * modes + m
                pr, pi = probes[u][m]
                dr = change[k * points : (k + 1) * points, :points]
                di = change[k * points : (k + 1) * points, points:]
                tr, ti = pr * dr + pi * di, pr * di - pi * dr
                term_r = tr if m == 0 else term_r + tr
                term_i = ti if m == 0 else term_i + ti
                part[slot, 2 * m] += wr * dr + wi * di
                part[slot, 2 * m + 1] += wr * di - wi * dr
            part[slot, 2 * modes] += (wr * wr + wi * wi) * flags[u]
            first = lane >= shift
            for ch, term in enumerate((term_r, term_i)):
                term = pltpu.roll(term, shift, 1)
                acc[ch, block, pl.ds(row, points), :] += jnp.where(first, term, 0.0)
                acc[ch, block + 1, pl.ds(row, points), :] += jnp.where(first, 0.0, term)
        return carry

    lax.fori_loop(0, (count + SLOTS_AT_ONCE - 1) // SLOTS_AT_ONCE, step, 0)

    copies = []
    at = 0
    for k, size in enumerate(group_sizes):
        copies.append(pltpu.make_async_copy(part.at[pl.ds(at, size)], groups[k], out_sems.at[k]))
        at += size
    k = len(group_sizes)
    copies.append(
        pltpu.make_async_copy(acc.at[:, pl.ds(0, blocks), pl.ds(tile_rows, points), :], num_low, out_sems.at[k])
    )
    copies.append(
        pltpu.make_async_copy(acc.at[:, pl.ds(0, blocks), pl.ds(0, tile_rows), :], num_top, out_sems.at[k + 1])
    )
    for copy in copies:
        copy.start()
    for copy in copies:
        copy.wait()


def update(meta, slot_of, live, amplitudes, obj, rim, factors, pieces, group_sizes):
    points = amplitudes.shape[-1]
    tile_rows = obj.shape[1]
    blocks = obj.shape[2] // LANES
    channels = pieces[0].shape[1]
    scans = slot_of.shape[0]
    piece_sizes = tuple(piece.shape[0] for piece in pieces)
    slots = sum(piece_sizes)
    f32 = jnp.float32
    smem = pl.BlockSpec(memory_space=pltpu.SMEM)
    vmem = pl.BlockSpec(memory_space=pltpu.VMEM)
    anywhere = pl.BlockSpec(memory_space=pl.ANY)
    return pl.pallas_call(
        functools.partial(update_kernel, (piece_sizes, group_sizes, slots)),
        out_shape=[
            jax.ShapeDtypeStruct((2, blocks, tile_rows, LANES), f32),
            jax.ShapeDtypeStruct((2, blocks, points, LANES), f32),
            jax.ShapeDtypeStruct((scans, points, points), f32),
        ]
        + [jax.ShapeDtypeStruct((size, channels + 1, points, points), f32) for size in group_sizes],
        in_specs=[smem] * 3 + [vmem, anywhere, anywhere, vmem] + [anywhere] * len(pieces),
        out_specs=[anywhere, anywhere, vmem] + [anywhere] * len(group_sizes),
        scratch_shapes=[
            pltpu.VMEM((slots, channels, points, points), f32),
            pltpu.VMEM((2, blocks + 1, tile_rows + points, LANES), f32),
            pltpu.VMEM((2, blocks + 1, tile_rows + points, LANES), f32),
            pltpu.VMEM((slots, channels + 1, points, points), f32),
            pltpu.SemaphoreType.DMA((len(pieces) + 2 * blocks,)),
            pltpu.SemaphoreType.DMA((len(group_sizes) + 2,)),
        ],
        compiler_params=pltpu.CompilerParams(vmem_limit_bytes=VMEM_BYTES),
        cost_estimate=pl.CostEstimate(flops=6 * 10**9, bytes_accessed=16 * 2**20, transcendentals=2**18),
        name="update",
    )(meta, slot_of, live, amplitudes, obj, rim, factors, *pieces)


def density_kernel(meta, above, squares, obj, num_top, out, scale, ext):
    points = LANES
    tile_rows = obj.shape[1]
    blocks = scale.shape[0]
    ext[...] = jnp.zeros_like(ext)
    lane = lax.broadcasted_iota(jnp.int32, (points, LANES), 1)

    def place(values, row, col):
        block, shift = col // LANES, col % LANES
        first = lane >= shift
        values = pltpu.roll(values, shift, 1)
        ext[block, pl.ds(row, points), :] += jnp.where(first, values, 0.0)
        ext[block + 1, pl.ds(row, points), :] += jnp.where(first, 0.0, values)

    def own(p, carry):
        @pl.when(meta[4 * p + 3] > 0)
        def _():
            place(squares[meta[4 * p + 2]], meta[4 * p] + points, meta[4 * p + 1])

        return carry

    def upper(p, carry):
        row = above[4 * p] - tile_rows + points

        @pl.when((above[4 * p + 3] > 0) & (row > 0))
        def _():
            place(squares[above[4 * p + 2]], row, above[4 * p + 1])

        return carry

    lax.fori_loop(0, meta.shape[0] // 4, own, 0)
    lax.fori_loop(0, above.shape[0] // 4, upper, 0)
    for b in range(blocks):
        columns = slice(b * LANES, (b + 1) * LANES)
        scale[b] = 1.0 / (ext[b, points : 2 * points, :] + damping)
        lower = 1.0 / (ext[b, 2 * points : points + tile_rows, :] + damping)
        for ch in range(2):
            out[ch, points:, columns] = obj[ch, points:, columns] + num_top[ch, b, points:] * lower
            out[ch, :points, columns] = obj[ch, :points, columns]


def density_of(meta, above, squares, obj, num_top):
    points = squares.shape[-1]
    blocks, tile_rows = num_top.shape[1:3]
    smem = pl.BlockSpec(memory_space=pltpu.SMEM)
    vmem = pl.BlockSpec(memory_space=pltpu.VMEM)
    return pl.pallas_call(
        density_kernel,
        out_shape=[
            jax.ShapeDtypeStruct(obj.shape, jnp.float32),
            jax.ShapeDtypeStruct((blocks, points, LANES), jnp.float32),
        ],
        in_specs=[smem, smem, vmem, vmem, vmem],
        out_specs=[vmem, vmem],
        scratch_shapes=[pltpu.VMEM((blocks + 1, points + tile_rows + points, LANES), jnp.float32)],
        compiler_params=pltpu.CompilerParams(vmem_limit_bytes=VMEM_BYTES),
        cost_estimate=pl.CostEstimate(flops=2**23, bytes_accessed=8 * 2**20, transcendentals=0),
        name="density",
    )(meta, above, squares, obj, num_top)


def finish_kernel(begun, num_top, received, scale, out):
    for b in range(scale.shape[0]):
        columns = slice(b * LANES, (b + 1) * LANES)
        for ch in range(2):
            out[ch, :, columns] = begun[ch, :, columns] + (num_top[ch, b] + received[ch, b]) * scale[b]


def finish(begun, num_top, received, scale):
    blocks, points = scale.shape[:2]
    whole = pl.BlockSpec(memory_space=pltpu.VMEM)
    rows = pl.BlockSpec((2, points, begun.shape[2]), lambda i: (0, 0, 0))
    head = pl.BlockSpec((2, blocks, points, LANES), lambda i: (0, 0, 0, 0))
    return pl.pallas_call(
        finish_kernel,
        grid=(1,),
        out_shape=jax.ShapeDtypeStruct(begun.shape, begun.dtype),
        in_specs=[rows, head, head, pl.BlockSpec((blocks, points, LANES), lambda i: (0, 0, 0))],
        out_specs=rows,
        input_output_aliases={0: 0},
        compiler_params=pltpu.CompilerParams(vmem_limit_bytes=VMEM_BYTES),
        cost_estimate=pl.CostEstimate(flops=2**20, bytes_accessed=5 * 2**20, transcendentals=0),
        name="finish",
    )(begun, num_top, received, scale)


def staged_kernel(*refs):
    half = (len(refs) - 1) // 2
    copies = [pltpu.make_async_copy(refs[k], refs[half + k], refs[-1].at[k]) for k in range(half)]
    for copy in copies:
        copy.start()
    for copy in copies:
        copy.wait()


def staged(*arrays):
    return pl.pallas_call(
        staged_kernel,
        out_shape=[jax.ShapeDtypeStruct(array.shape, array.dtype) for array in arrays],
        in_specs=[pl.BlockSpec(memory_space=pl.ANY)] * len(arrays),
        out_specs=[pl.BlockSpec(memory_space=pltpu.VMEM)] * len(arrays),
        scratch_shapes=[pltpu.SemaphoreType.DMA((len(arrays),))],
        compiler_params=pltpu.CompilerParams(vmem_limit_bytes=VMEM_BYTES),
        name="staged",
    )(*arrays)


def local(object_strip, probe_store, amplitudes, scan_of, offsets, counts, owner):
    device = lax.axis_index("row")
    size = lax.axis_size("row")
    tile_rows = object_strip.shape[1]
    points = probe_store.shape[-1]
    modes = probe_store.shape[1]
    slot_count = amplitudes.shape[0]
    scan_count = owner.shape[0]
    channels = 2 * modes
    swaps = size == 16
    own_probe = probe_store.reshape(1, channels, points, points)

    is_live = (jnp.arange(slot_count, dtype=jnp.int32) < counts[0]).astype(jnp.int32)
    meta = jnp.stack([offsets[:, 0] - device * tile_rows, offsets[:, 1], scan_of, is_live], axis=1).reshape(-1)

    if swaps:
        held = {0: own_probe}
        for key in (8, 4, 2):
            held[key] = swapped(own_probe, key)
        held[8], held[4], held[2] = lax.optimization_barrier((held[8], held[4], held[2]))
        held[6] = swapped(held[2], 4)
        held[12] = swapped(held[8], 4)
        held[10] = swapped(held[8], 2)
        held[14] = swapped(held[10], 4)
        for key in list(held):
            held[key | 1] = swapped(held[key], 1)
        order = [key | core for core in (0, 1) for key in FAR + NEAR]
        amplitudes, factors, held[0] = staged(amplitudes, after(transform_tables(points), held[12]), own_probe)
        pieces = [held[key] for key in order]
        key = jnp.bitwise_xor(owner, device)
        side = key // 2 % 4
        slot_of = key % 2 * 8 + (1 - key // 8) * 4 + jnp.bitwise_xor(side, side // 2)
        group_sizes = (4,) * 4
    else:
        owned = (owner == device)[:, None, None, None]
        pieces = [lax.psum(jnp.where(owned, own_probe, 0.0), "row")]
        slot_of = jnp.arange(scan_count, dtype=jnp.int32)
        group_sizes = (scan_count,)
        factors = transform_tables(points)

    rim = moved(after(object_strip[:, :points, :], slot_of), -1)
    above = moved(after(meta, held[7]) if swaps else meta, 1)
    rim = after(rim, above)
    num_top, num_low, squares, *groups = update(
        meta, slot_of, counts, amplitudes, object_strip, rim, factors, pieces, group_sizes
    )

    begun, scale = density_of(meta, above, squares, object_strip, num_top)
    if swaps:
        mine_far, mine_near, theirs_far, theirs_near = groups
        total, received, scale = reduced((mine_far, swapped(theirs_far, 1)), theirs_near, mine_near, num_low, scale)
    else:
        received = moved(num_low, 1)
        summed = lax.psum(groups[0], "row")
        total = jnp.sum(jnp.where(owned, summed, 0.0), axis=0)
    new_object = finish(begun, num_top, received, scale)
    new_probes = own_probe[0] + total[:channels] / (total[channels] + damping)
    return (new_object, new_probes.reshape(probe_store.shape))


def solution(mesh):
    return jax.shard_map(
        local,
        mesh=mesh,
        in_specs=(
            P(None, ("grp", "row"), None),
            P(("grp", "row"), None, None, None, None),
            P(("grp", "row"), None, None),
            P(("grp", "row")),
            P(("grp", "row"), None),
            P(("grp", "row")),
            P("grp"),
        ),
        out_specs=(P(None, ("grp", "row"), None), P(("grp", "row"), None, None, None, None)),
        check_vma=False,
    )
```
